32 devices in a mesh: ctx: 8 (over y, x, core), ch: 4 (over z).
Axes of the slice: x: 2, y: 2, z: 4, core: 2. Of those that a mesh axis runs over, the one named last changes fastest.
Arguments:
- gate_query: bfloat16 [2048, 8192], P('ctx', 'ch'), may hold values from -6 to 6
- gate_key: bfloat16 [2048, 8192], P('ctx', 'ch'), may hold values from -6 to 6
- value_in: bfloat16 [2048, 8192], P('ctx', 'ch'), may hold values from -6 to 6
- mr_filter: bfloat16 [128, 512], P(None, 'ch'), may hold values from -0.5 to 0.5
- pole_rates: float32 [16, 512], P(None, 'ch'), may hold values from 2.4414063e-05 to 0.05
- residues: float32 [16, 512], P(None, 'ch'), may hold values from -3 to 3
- skip_gain: float32 [8192], P('ch'), may hold values from -4 to 4
- offsets: int32 [65], replicated, may hold values from 0 to 2048, as said below
- owner_docs: int32 [32], replicated, may hold values from 0 to 63, as said below
Outputs:
- output: bfloat16 [2048, 8192], P('ctx', 'ch')
- doc_states: float32 [32, 16, 8192], P(('ctx', 'ch'))
The draws below stay inside these ranges and needn't reach their ends.
Inputs may be any that keep to these rules, and one draw needn't show every extreme that they name: offsets[0] = 0 and offsets[64] = 2048, strictly increasing; document d holds tokens offsets[d] to offsets[d + 1] - 1. The last tokens of at most 16 documents lie among the 256 tokens of one index of ctx, and some index holds exactly 16. `owner_docs`: for some base b, slot r * 4 + k (k < 4) holds document (b + k * 8 + r) mod 64.
All inputs are finite; a program needn't handle non-finite values.
Results may differ from the reference program's by a relative error of at most 0.0049.
Values may be sent and summed in bfloat16 or wider, within the bound.
No kernel may reach another device: no remote copies, remote signals or barrier semaphores. Data moves between devices by JAX's collectives and lax.ppermute only.
A program may use at most 320 MiB of HBM per device.

```python
import math
import jax
import jax.numpy as jnp
from jax import lax

D = 8192
NPOLE = 16
MR_LEN = 128
TOK_DEV = 256
DOC_CTX = 8
NGROUP = 512
TOKENS = 2048
NDOC = 64
ENDS = 16
NSEL = 32


def draw_offsets(key, part):
    first_key, second_key = jax.random.split(jax.random.fold_in(key, 11))
    devices_count = TOKENS // TOK_DEV
    quarter = devices_count // 4
    base_counts = jnp.concatenate([jnp.zeros((quarter,), jnp.int32), jnp.full((quarter,), 2 * DOC_CTX, jnp.int32), jnp.full((devices_count - 2 * quarter,), DOC_CTX, jnp.int32)])
    counts = base_counts[jax.random.permutation(first_key, devices_count)]
    first_full = jnp.argmax((counts > 0).astype(jnp.int32))
    counts = jnp.roll(counts, devices_count - 1 - first_full)
    device_keys = jax.random.split(second_key, devices_count)
    orders = jax.vmap(lambda one_key: jax.random.permutation(one_key, TOK_DEV - 1))(device_keys)
    chosen_pos = orders[:, :ENDS].astype(jnp.int32)
    chosen_pos = chosen_pos.at[devices_count - 1, 0].set(TOK_DEV - 1)
    slot_ids = jnp.arange(ENDS, dtype=jnp.int32)
    valid = slot_ids[None, :] < counts[:, None]
    global_pos = jnp.arange(devices_count, dtype=jnp.int32)[:, None] * TOK_DEV + chosen_pos
    global_pos = jnp.where(valid, global_pos, TOKENS + 1)
    end_list = jnp.sort(global_pos.reshape(-1))[:NDOC]
    return jnp.concatenate([jnp.zeros((1,), jnp.int32), end_list + 1]).astype(jnp.int32)


def draw_owner_docs(key, part):
    devices_count = TOKENS // TOK_DEV
    per_owner = NSEL // devices_count
    base = jax.random.randint(jax.random.fold_in(key, 23), (), 0, NDOC).astype(jnp.int32)
    slot_ids = jnp.arange(NSEL, dtype=jnp.int32)
    owner_rank = slot_ids // per_owner
    local_slot = slot_ids % per_owner
    return ((base + local_slot * devices_count + owner_rank) % NDOC).astype(jnp.int32)


def levels(rng, shape, shards, least, high):
    def one(dim, blocks):
        heights = jax.random.uniform(jax.random.fold_in(jax.random.fold_in(rng, 6), dim), (blocks,), jnp.float32, least / len(shards), high / len(shards))
        return jnp.repeat(jnp.exp(heights), shape[dim] // blocks).reshape((-1,) + (1,) * (len(shape) - dim - 1))

    factor_of = one(*shards[0])
    for cut in shards[1:]:
        factor_of = factor_of * one(*cut)
    return factor_of


def centred(rng, shape, scale, most, cuts=(), kind=jnp.bfloat16):
    array = jax.random.normal(rng, shape, jnp.float32) * scale
    if len(cuts) > 0:
        array = levels(rng, shape, cuts, -0.22, 0.18) * array
    return jnp.clip(array, min=-most, max=most).astype(kind)


def setup_inputs(seed: int = 0) -> dict:
    key_list = jax.random.split(jax.random.key(seed), 10)
    return {
        "gate_query": centred(key_list[0], (TOKENS, D), 1.0, 6.0, ((0, 8), (1, 4))),
        "gate_key": centred(key_list[1], (TOKENS, D), 1.0, 6.0, ((0, 8), (1, 4))),
        "value_in": centred(key_list[2], (TOKENS, D), 1.0, 6.0, ((0, 8), (1, 4))),
        "mr_filter": centred(key_list[3], (MR_LEN, NGROUP), MR_LEN ** -0.5, 0.5, ((1, 4),)),
        "pole_rates": jnp.clip(jnp.exp(math.log(0.05) - 7.624619 * jax.random.uniform(key_list[4], (NPOLE, NGROUP), jnp.float32) ** levels(key_list[4], (NPOLE, NGROUP), ((1, 4),), -0.2, 0.2)), 2.441406286379788e-05, 0.05),
        "residues": centred(key_list[5], (NPOLE, NGROUP), 0.5, 3.0, ((1, 4),), jnp.float32),
        "skip_gain": centred(key_list[6], (D,), 1.0, 4.0, ((0, 4),), jnp.float32),
        "offsets": draw_offsets(jax.random.fold_in(key_list[9], 71), 0),
        "owner_docs": draw_owner_docs(jax.random.fold_in(key_list[9], 71), 0),
    }


highest = lax.Precision.HIGHEST

def reference(gate_query, gate_key, value_in, mr_filter, pole_rates, residues, skip_gain, offsets, owner_docs):
    total_len = gate_query.shape[0]
    width = gate_query.shape[1]
    pole_count = pole_rates.shape[0]
    groups = pole_rates.shape[1]
    group_size = width // groups
    blocks = total_len // MR_LEN
    positions = jnp.arange(total_len, dtype=jnp.int32)
    doc_index = lax.optimization_barrier(jnp.sum((offsets[1:][None, :] <= positions[:, None]).astype(jnp.int32), axis=1))
    starts = jnp.take(offsets, doc_index).astype(jnp.int32)
    starts_blocked = starts.reshape(blocks, MR_LEN)
    row_ids = jnp.arange(MR_LEN, dtype=jnp.int32)
    col_ids = jnp.arange(2 * MR_LEN, dtype=jnp.int32)
    tap_lag = row_ids[:, None] + MR_LEN - col_ids[None, :]
    lag_valid = (tap_lag >= 0) & (tap_lag < MR_LEN)
    tap_table = jnp.take(mr_filter, jnp.clip(tap_lag, 0, MR_LEN - 1), axis=0)
    mr_kernel = jnp.where(lag_valid[:, :, None], tap_table, jnp.zeros_like(tap_table)).transpose(2, 0, 1)
    padded = jnp.concatenate([jnp.zeros((MR_LEN, width), value_in.dtype), value_in], axis=0)
    earlier = padded[:total_len].reshape(blocks, MR_LEN, width)
    current = value_in.reshape(blocks, MR_LEN, width)
    windows = jnp.concatenate([earlier, current], axis=1)
    block_ids = jnp.arange(blocks, dtype=jnp.int32)

    def mr_block(unused_carry, inputs):
        window, block_starts, block_id = inputs
        source = block_id * MR_LEN - MR_LEN + col_ids
        allowed = source[None, :] >= block_starts[:, None]
        masked = jnp.where(allowed[None], mr_kernel, jnp.zeros_like(mr_kernel))
        result = jnp.einsum('gij,jgc->igc', masked.astype(jnp.float32), window.reshape(2 * MR_LEN, groups, group_size).astype(jnp.float32), precision=highest)
        return (unused_carry, result.reshape(MR_LEN, width))
    unused_final, mr_out = lax.scan(mr_block, jnp.zeros((), jnp.float32), (windows, starts_blocked, block_ids))
    mr_out = mr_out.reshape(total_len, width)
    mixed = (gate_key.astype(jnp.float32) * mr_out).astype(jnp.bfloat16)
    step_range = jnp.arange(MR_LEN + 1, dtype=jnp.int32).astype(jnp.float32)
    powers = jnp.exp(-pole_rates[:, :, None] * step_range[None, None, :])
    scaling = jnp.sqrt(-jnp.expm1(-2.0 * pole_rates))
    li_taps = lax.optimization_barrier(jnp.sum((residues * scaling)[:, :, None] * powers[:, :, :MR_LEN], axis=0))
    tap_gap = row_ids[:, None] - row_ids[None, :]
    li_kernel = jnp.where((tap_gap >= 0)[None], jnp.take(li_taps, jnp.clip(tap_gap, 0, MR_LEN - 1), axis=1), 0.0)
    carry_in = powers[:, :, 1:MR_LEN + 1].transpose(2, 0, 1) * residues[None]
    feed_weights = scaling[:, :, None] * jnp.flip(powers[:, :, :MR_LEN], axis=2)
    block_decay = powers[:, :, MR_LEN]
    mixed_blocks = mixed.reshape(blocks, MR_LEN, width)

    def li_block(mode_state, inputs):
        block_vals, block_starts, block_id = inputs
        first_pos = block_id * MR_LEN
        values = block_vals.astype(jnp.float32).reshape(MR_LEN, groups, group_size)
        allowed = first_pos + row_ids[None, :] >= block_starts[:, None]
        inner_kernel = jnp.where(allowed[None], li_kernel, 0.0)
        local_out = jnp.einsum('gij,jgc->igc', inner_kernel, values, precision=highest)
        carried = (block_starts < first_pos).astype(jnp.float32)
        local_out = local_out + jnp.einsum('ing,ngc->igc', carry_in * carried[:, None, None], mode_state, precision=highest)
        tail_start = block_starts[MR_LEN - 1]
        take_in = (first_pos + row_ids >= tail_start).astype(jnp.float32)
        keep_gain = (tail_start < first_pos).astype(jnp.float32)
        new_state = block_decay[:, :, None] * mode_state * keep_gain + jnp.einsum('ngj,jgc->ngc', feed_weights * take_in[None, None, :], values, precision=highest)
        return (new_state, (local_out.reshape(MR_LEN, width), mode_state))
    start_state = jnp.zeros((pole_count, groups, group_size), jnp.float32)
    unused_state, (li_out, before) = lax.scan(li_block, start_state, (mixed_blocks, starts_blocked, block_ids))
    li_out = li_out.reshape(total_len, width)
    output = (gate_query.astype(jnp.float32) * (li_out + skip_gain[None, :] * mixed.astype(jnp.float32))).astype(jnp.bfloat16)

    def end_state(doc_number):
        doc_begin = offsets[doc_number]
        last_pos = offsets[doc_number + 1] - 1
        block_id = (last_pos // MR_LEN).astype(jnp.int32)
        inside = last_pos % MR_LEN
        first_pos = (block_id * MR_LEN).astype(jnp.int32)
        values = lax.dynamic_slice_in_dim(mixed, first_pos, MR_LEN, 0).astype(jnp.float32).reshape(MR_LEN, groups, group_size)
        distance = inside - row_ids
        usable = (distance >= 0) & (first_pos + row_ids >= doc_begin)
        weights = scaling[:, :, None] * jnp.exp(-pole_rates[:, :, None] * jnp.where(usable, distance, 0).astype(jnp.float32)[None, None, :]) * usable.astype(jnp.float32)[None, None, :]
        fresh_state = jnp.einsum('ngj,jgc->ngc', weights, values, precision=highest)
        prior_state = lax.dynamic_index_in_dim(before, block_id, 0, keepdims=False)
        link_gain = (doc_begin < first_pos).astype(jnp.float32) * jnp.exp(-pole_rates * (inside + 1).astype(jnp.float32))
        return (fresh_state + link_gain[:, :, None] * prior_state).reshape(pole_count, width)
    doc_states = lax.map(end_state, owner_docs)
    return (output, doc_states)
```

```python
import functools

import jax
import jax.numpy as jnp
from jax import lax
from jax.experimental import pallas as pl
from jax.experimental.pallas import tpu as pltpu
from jax.sharding import PartitionSpec as P

TAPS = 128
ENDS = 16
LANES = 128
F32 = jnp.float32
BF16 = jnp.bfloat16

SMEM = pl.BlockSpec(memory_space=pltpu.SMEM)


def params(grid_dims):
    return pltpu.CompilerParams(
        dimension_semantics=("arbitrary",) * grid_dims, vmem_limit_bytes=48 * 1024 * 1024
    )


def iota(shape, dim):
    return lax.broadcasted_iota(jnp.int32, shape, dim)


def dot(a, b):
    return lax.dot_general(a, b, (((1,), (0,)), ((), ())), preferred_element_type=F32)


def dot_t(a, b):
    return lax.dot_general(a, b, (((0,), (0,)), ((), ())), preferred_element_type=F32)


def spread(x, first_group, size, lanes):
    groups = x.shape[1]
    pick = (iota((groups, lanes), 0) == first_group + iota((groups, lanes), 1) // size).astype(F32)
    pick = pick.astype(BF16)
    high = x.astype(BF16)
    rest = x - high.astype(F32)
    mid = rest.astype(BF16)
    low = (rest - mid.astype(F32)).astype(BF16)
    return dot(high, pick) + dot(mid, pick) + dot(low, pick)


def circulant(row):
    return pltpu.roll(
        jnp.broadcast_to(row, (TAPS, TAPS)), 0, 1, stride=1, stride_axis=0
    ).astype(BF16)


def states_kernel(
    cap,
    size,
    offsets,
    owners,
    place,
    halo,
    value,
    key,
    filt,
    rates,
    gains,
    resid,
    mixed_out,
    ends_out,
    spread_out,
    masks_out,
    taps_out,
    filter_rows,
    picks,
    flat,
    first_tok,
    last_tok,
):
    length = value.shape[0]
    poles, groups = rates.shape
    docs = offsets.shape[0] - 1
    peers = ends_out.shape[0]
    slots = owners.shape[0] // peers
    rows = peers * cap
    padded = picks.shape[0]
    tile = pl.program_id(0)
    per_tile = LANES // size
    begin = place[0] * length

    @pl.when(tile == 0)
    def prepare():
        spot = begin + iota((length, LANES), 0)

        def at(d, carry):
            off = offsets[d]
            return (
                jnp.where(spot >= off, off, carry[0]),
                jnp.where(off <= begin + length - 1, off, carry[1]),
            )

        starts, last_start = lax.fori_loop(
            0, docs, at, (jnp.zeros((length, LANES), jnp.int32), jnp.int32(0))
        )
        i, j = iota((TAPS, TAPS), 0), iota((TAPS, TAPS), 1)
        s0, s1 = starts[:TAPS], starts[TAPS:]
        cross = s1 <= begin + j
        for index, mask in enumerate(
            (
                (j > i) & (s0 <= begin - TAPS + j),
                (j <= i) & (s0 <= begin + j),
                (j > i) & cross,
                (j <= i) & (s1 <= begin + TAPS + j),
                (j <= i) & cross,
            )
        ):
            masks_out[index] = mask.astype(F32).astype(BF16)
        turn = (i == (TAPS - j) % TAPS).astype(F32).astype(BF16)
        filter_rows[...] = dot_t(filt[...], turn)
        lag = iota((TAPS, groups), 0).astype(F32)
        for half in range(2):
            total = jnp.zeros((TAPS, groups), F32)
            for n in range(poles):
                total = total + (resid[n : n + 1] * gains[n : n + 1]) * jnp.exp(
                    -rates[n : n + 1] * (lag + float(half * TAPS))
                )
            taps_out[half] = dot_t(total.astype(BF16), turn)

        first_tok[rows] = jnp.maximum(last_start - begin, 0)
        last_tok[rows] = length - 1
        for s in range(rows):
            r, parity = s // cap, s % cap

            def look(h, found, r=r, parity=parity):
                doc = owners[r * slots + h * cap + parity]
                end = offsets[doc + 1] - 1 - begin
                here = (end >= 0) & (end < length)
                return (
                    jnp.where(here, jnp.maximum(offsets[doc] - begin, 0), found[0]),
                    jnp.where(here, end, found[1]),
                )

            got = lax.fori_loop(0, slots // cap, look, (jnp.int32(1), jnp.int32(0)))
            first_tok[s] = got[0]
            last_tok[s] = got[1]
        row = iota((padded, length), 0)
        low = jnp.ones((padded, length), jnp.int32)
        high = jnp.zeros((padded, length), jnp.int32)
        for s in range(rows + 1):
            low = jnp.where(row == s, first_tok[s], low)
            high = jnp.where(row == s, last_tok[s], high)
        token = iota((padded, length), 1)
        picks[...] = ((token >= low) & (token <= high)).astype(F32).astype(BF16)

    group_rows = filter_rows[pl.ds(tile * per_tile, per_tile), :]
    window0 = jnp.concatenate([halo[...], value[:TAPS]], axis=0)
    window1 = value[...]
    lane_group = iota((TAPS, LANES), 1) // size
    acc0 = jnp.zeros((TAPS, LANES), F32)
    acc1 = jnp.zeros((TAPS, LANES), F32)
    for g in range(per_tile):
        c = circulant(group_rows[g : g + 1])
        y0 = dot(jnp.concatenate([c * masks_out[0], c * masks_out[1]], axis=1), window0)
        y1 = dot(jnp.concatenate([c * masks_out[2], c * masks_out[3]], axis=1), window1)
        acc0 = jnp.where(lane_group == g, y0, acc0)
        acc1 = jnp.where(lane_group == g, y1, acc1)
    mixed = (key[...].astype(F32) * jnp.concatenate([acc0, acc1], axis=0)).astype(BF16)
    mixed_out[...] = mixed
    wide = mixed.astype(F32)

    p = spread(rates[...], tile * per_tile, size, LANES)
    beta = spread(gains[...], tile * per_tile, size, LANES)
    spread_out[...] = p
    step = 16
    near = iota((step, LANES), 0).astype(F32)
    for n in range(poles):
        pn = p[n : n + 1]
        grow = jnp.exp(pn * near)
        jump = jnp.broadcast_to(jnp.exp(pn * float(step)), (step, LANES))
        parts = []
        for k in range(length // step):
            parts.append((grow * wide[k * step : (k + 1) * step]).astype(BF16))
            grow = grow * jump
        flat[n * padded : (n + 1) * padded, :] = dot(picks[...], jnp.concatenate(parts, axis=0))
    for s in range(rows + 1):
        state = flat[pl.ds(s, poles, stride=padded), :]
        state = state * jnp.exp(-p * last_tok[s].astype(F32)) * beta
        state = state.astype(BF16)
        if s < rows:
            ends_out[s // cap, s % cap] = state
        else:
            for r in range(peers):
                ends_out[r, cap] = state


def local_kernel(size, mixed, masks, taps, skip, local_out):
    tile = pl.program_id(0)
    per_tile = LANES // size
    rows_a = taps[0, pl.ds(tile * per_tile, per_tile), :]
    rows_b = taps[1, pl.ds(tile * per_tile, per_tile), :]
    lane_group = iota((TAPS, LANES), 1) // size
    acc0 = jnp.zeros((TAPS, LANES), F32)
    acc1 = jnp.zeros((TAPS, LANES), F32)
    x = mixed[...]
    for g in range(per_tile):
        a, b = circulant(rows_a[g : g + 1]), circulant(rows_b[g : g + 1])
        y0 = dot(a * masks[1], x[:TAPS])
        y1 = dot(jnp.concatenate([a * masks[2] + b * masks[4], a * masks[3]], axis=1), x)
        acc0 = jnp.where(lane_group == g, y0, acc0)
        acc1 = jnp.where(lane_group == g, y1, acc1)
    local_out[...] = jnp.concatenate([acc0, acc1], axis=0) + skip[...] * x.astype(F32)


def slots_kernel(length, offsets, owners, place, got, rates, slot_out, entering_out):
    peers, cap = got.shape[0], got.shape[1] - 1
    slots = slot_out.shape[0]
    docs = offsets.shape[0] - 1
    me = place[0]
    p = rates[...]
    fade = jnp.exp(-p * float(length))

    def entering(first, stop):
        def hop(c, state):
            return fade * state + got[c, cap].astype(F32)

        return lax.fori_loop(first, stop, hop, jnp.zeros(p.shape, F32))

    def at(d, start):
        return jnp.where(offsets[d] <= me * length, offsets[d], start)

    my_start = lax.fori_loop(0, docs, at, jnp.int32(0))
    entering_out[...] = entering(my_start // length, me)
    for k in range(slots):
        doc = owners[me * slots + k]
        start, end = offsets[doc], offsets[doc + 1] - 1
        source = end // length
        gain = jnp.exp(-p * (end - source * length + 1).astype(F32))
        state = got[source, k % cap].astype(F32) + gain * entering(start // length, source)
        slot_out[k] = state.astype(BF16)


def output_kernel(length, size, offsets, place, query, local, entering, rates, resid, out):
    docs = offsets.shape[0] - 1
    begin = place[0] * length
    poles, width = entering.shape

    def at(d, limit):
        return jnp.where(
            (offsets[d] < begin) & (offsets[d + 1] > begin), offsets[d + 1] - begin, limit
        )

    limit = lax.fori_loop(0, docs, at, jnp.int32(0))
    t = iota((length, width), 0)
    weight = jnp.exp(-rates[...] * (t + 1).astype(F32)) * resid[...]
    weight = jnp.where(t < limit, weight, 0.0)
    w_high = weight.astype(BF16)
    w_low = (weight - w_high.astype(F32)).astype(BF16)
    e = entering[...]
    e_high = e.astype(BF16)
    e_low = (e - e_high.astype(F32)).astype(BF16)
    kept = iota((width, width), 0) // poles == iota((width, width), 1) // size
    kept = kept.astype(F32).astype(BF16)
    b_high = jnp.concatenate([e_high] * (width // size), axis=0) * kept
    b_low = jnp.concatenate([e_low] * (width // size), axis=0) * kept
    fix = dot(w_high, b_high) + dot(w_low, b_high) + dot(w_high, b_low)
    out[...] = (query[...].astype(F32) * (local[...] + fix)).astype(BF16)


def widen_kernel(x, out):
    out[...] = x[...].astype(F32)


def per_device(query, key, value, filt, rates, resid, skip, offsets, owners):
    length, width = value.shape
    poles, groups = rates.shape
    size = width // groups
    peers, lines = lax.axis_size("ctx"), lax.axis_size("ch")
    slots = owners.shape[0] // peers
    cap = -(-ENDS // peers)
    rows = peers * cap
    padded = -(-(rows + 1) // 16) * 16
    place = lax.axis_index("ctx").astype(jnp.int32).reshape(1)
    gains = jnp.sqrt(-jnp.expm1(-2.0 * rates))
    rates_flat = rates.T.reshape(1, groups * poles)
    resid_flat = resid.T.reshape(1, groups * poles)

    halo = lax.ppermute(
        value[length - TAPS :], "ctx", [(i, i + 1) for i in range(peers - 1)]
    )

    def whole(shape):
        return pl.BlockSpec(shape, lambda i: (0,) * len(shape))

    def lanes(height, w=LANES):
        return pl.BlockSpec((height, w), lambda i: (0, i))

    mixed, ends, rates_wide, masks, taps = pl.pallas_call(
        functools.partial(states_kernel, cap, size),
        grid=(width // LANES,),
        in_specs=[
            SMEM,
            SMEM,
            SMEM,
            lanes(TAPS),
            lanes(length),
            lanes(length),
            whole((TAPS, groups)),
            whole((poles, groups)),
            whole((poles, groups)),
            whole((poles, groups)),
        ],
        out_specs=[
            lanes(length),
            pl.BlockSpec((peers, cap + 1, poles, LANES), lambda i: (0, 0, 0, i)),
            lanes(poles),
            whole((5, TAPS, TAPS)),
            whole((2, groups, TAPS)),
        ],
        out_shape=[
            jax.ShapeDtypeStruct((length, width), BF16),
            jax.ShapeDtypeStruct((peers, cap + 1, poles, width), BF16),
            jax.ShapeDtypeStruct((poles, width), F32),
            jax.ShapeDtypeStruct((5, TAPS, TAPS), BF16),
            jax.ShapeDtypeStruct((2, groups, TAPS), F32),
        ],
        scratch_shapes=[
            pltpu.VMEM((groups, TAPS), F32),
            pltpu.VMEM((padded, length), BF16),
            pltpu.VMEM((poles * padded, LANES), F32),
            pltpu.SMEM((padded,), jnp.int32),
            pltpu.SMEM((padded,), jnp.int32),
        ],
        compiler_params=params(1),
        name="states",
    )(offsets, owners, place, halo, value, key, filt, rates, gains, resid)

    got = lax.all_to_all(ends, "ctx", split_axis=0, concat_axis=0, tiled=True)

    local = pl.pallas_call(
        functools.partial(local_kernel, size),
        grid=(width // LANES,),
        in_specs=[
            lanes(length),
            whole((5, TAPS, TAPS)),
            whole((2, groups, TAPS)),
            lanes(1),
        ],
        out_specs=lanes(length),
        out_shape=jax.ShapeDtypeStruct((length, width), F32),
        compiler_params=params(1),
        cost_estimate=pl.CostEstimate(
            flops=2 * 2 * length * length * width * 8, bytes_accessed=6 * length * width, transcendentals=0
        ),
        name="local",
    )(mixed, masks, taps, skip.reshape(1, width))

    picked, entering = pl.pallas_call(
        functools.partial(slots_kernel, length),
        in_specs=[SMEM, SMEM, SMEM] + [pl.BlockSpec(memory_space=pltpu.VMEM)] * 2,
        out_specs=[pl.BlockSpec(memory_space=pltpu.VMEM)] * 2,
        out_shape=[
            jax.ShapeDtypeStruct((slots, poles, width), BF16),
            jax.ShapeDtypeStruct((poles, width), F32),
        ],
        compiler_params=params(0),
        name="slots",
    )(offsets, owners, place, got, rates_wide)

    gathered = lax.all_to_all(picked, "ch", split_axis=0, concat_axis=0, tiled=True)

    tile = 2 * LANES
    output = pl.pallas_call(
        functools.partial(output_kernel, length, size),
        grid=(width // tile,),
        in_specs=[
            SMEM,
            SMEM,
            lanes(length, tile),
            lanes(length, tile),
            lanes(poles, tile),
            lanes(1, tile),
            lanes(1, tile),
        ],
        out_specs=lanes(length, tile),
        out_shape=jax.ShapeDtypeStruct((length, width), BF16),
        compiler_params=params(1),
        cost_estimate=pl.CostEstimate(
            flops=6 * length * tile * width, bytes_accessed=8 * length * width, transcendentals=0
        ),
        name="output",
    )(offsets, place, query, local, entering, rates_flat, resid_flat)

    per_line = slots // lines
    doc_states = pl.pallas_call(
        widen_kernel,
        grid=(lines,),
        in_specs=[pl.BlockSpec((per_line, poles, width), lambda h: (h, 0, 0))],
        out_specs=pl.BlockSpec((per_line, poles, width), lambda h: (0, 0, h)),
        out_shape=jax.ShapeDtypeStruct((per_line, poles, lines * width), F32),
        compiler_params=params(1),
        name="widen",
    )(gathered)
    return (output, doc_states)


def solution(mesh):
    placed = (
        P("ctx", "ch"),
        P("ctx", "ch"),
        P("ctx", "ch"),
        P(None, "ch"),
        P(None, "ch"),
        P(None, "ch"),
        P("ch"),
        P(),
        P(),
    )
    return jax.shard_map(
        per_device,
        mesh=mesh,
        in_specs=placed,
        out_specs=(P("ctx", "ch"), P(("ctx", "ch"), None, None)),
        check_vma=False,
    )
```

```python
import functools

import jax
import jax.numpy as jnp
from jax import lax
from jax.experimental import pallas as pl
from jax.experimental.pallas import tpu as pltpu
from jax.sharding import PartitionSpec as P

TAPS = 128
ENDS = 16
LANES = 128
BLOCK = 512
PART = 512
CHUNK = 16
F32 = jnp.float32
BF16 = jnp.bfloat16

SMEM = pl.BlockSpec(memory_space=pltpu.SMEM)


def params(grid_dims):
    return pltpu.CompilerParams(
        dimension_semantics=("arbitrary",) * grid_dims, vmem_limit_bytes=60 * 1024 * 1024
    )


def iota(shape, dim):
    return lax.broadcasted_iota(jnp.int32, shape, dim)


def dot(a, b):
    return lax.dot_general(a, b, (((1,), (0,)), ((), ())), preferred_element_type=F32)


def dot_t(a, b):
    return lax.dot_general(a, b, (((0,), (0,)), ((), ())), preferred_element_type=F32)


def spread(x, first_group, size, lanes):
    groups = x.shape[1]
    pick = (iota((groups, lanes), 0) == first_group + iota((groups, lanes), 1) // size).astype(F32)
    pick = pick.astype(BF16)
    high = x.astype(BF16)
    rest = x - high.astype(F32)
    mid = rest.astype(BF16)
    low = (rest - mid.astype(F32)).astype(BF16)
    return dot(high, pick) + dot(mid, pick) + dot(low, pick)


def gain(rates):
    x = 2.0 * rates
    tail = 1.0 - x / 9.0
    for k in range(8, 1, -1):
        tail = 1.0 - x * tail * (1.0 / k)
    return jnp.sqrt(x * tail)


def circulant(row):
    return pltpu.roll(
        jnp.broadcast_to(row, (TAPS, TAPS)), 0, 1, stride=1, stride_axis=0
    ).astype(BF16)


def doc_at(offsets, position):
    docs = offsets.shape[0] - 1
    low, high = jnp.int32(0), jnp.int32(docs)
    for _ in range(docs.bit_length()):
        middle = (low + high) // 2
        left = offsets[middle] <= position
        low, high = jnp.where(left, middle, low), jnp.where(left, high, middle)
    return low


def filtered(blocks, masks, earlier, current, window, key):
    lane_group = iota((TAPS, LANES), 1) // (LANES // len(blocks))
    total = jnp.zeros((TAPS, LANES), F32)
    for g, c in enumerate(blocks):
        y = dot(jnp.concatenate([c * masks[earlier], c * masks[current]], axis=1), window)
        total = jnp.where(lane_group == g, y, total)
    return (key.astype(F32) * total).astype(BF16)


def prepare_kernel(
    cap,
    peers,
    size,
    offsets,
    owners,
    place,
    filt,
    rates,
    resid,
    rates_out,
    gains_out,
    rows_out,
    masks_out,
    taps_out,
    events,
):
    poles, groups = rates.shape
    width = rates_out.shape[1]
    length = 2 * TAPS
    docs = offsets.shape[0] - 1
    chosen = owners.shape[0]
    begin = place[0] * length
    d0 = doc_at(offsets, begin)

    def clear(t, carry):
        for u in range(8):
            events[t * 8 + u] = 0
        return carry

    lax.fori_loop(0, events.shape[0] // 8, clear, 0)

    def mark(k, carry):
        doc = d0 + k
        row = lax.rem(doc - owners[0] + docs, docs)
        start = offsets[jnp.minimum(doc, docs)] - begin
        last = offsets[jnp.minimum(doc + 1, docs)] - 1 - begin

        @pl.when((doc < docs) & (start >= 0) & (start < length))
        def opens():
            events[start] += 1
            events[length + start // CHUNK] = 1

        @pl.when((doc < docs) & (last < length) & (row < chosen))
        def closes():
            spot = lax.rem(row, peers) * cap + lax.rem(row // peers, cap)
            events[last] += 2 + 2 * spot
            events[length + last // CHUNK] = 1

        return carry

    lax.fori_loop(0, ENDS + 1, mark, 0)

    spot = begin + iota((length, LANES), 0)
    starts = jnp.broadcast_to(offsets[d0], (length, LANES))
    for k in range(1, ENDS + 1):
        off = offsets[jnp.minimum(d0 + k, docs)]
        starts = jnp.where(spot >= off, off, starts)
    i, j = iota((TAPS, TAPS), 0), iota((TAPS, TAPS), 1)
    s0, s1 = starts[:TAPS], starts[TAPS:]
    cross = s1 <= begin + j
    for index, mask in enumerate(
        (
            (j > i) & (s0 <= begin - TAPS + j),
            (j <= i) & (s0 <= begin + j),
            (j > i) & cross,
            (j <= i) & (s1 <= begin + TAPS + j),
            (j <= i) & cross,
        )
    ):
        masks_out[index] = mask.astype(F32).astype(BF16)
    turn = (i == (TAPS - j) % TAPS).astype(F32).astype(BF16)
    rows_out[...] = dot_t(filt[...], turn)
    lag = iota((TAPS, groups), 0).astype(F32)
    gains = gain(rates[...])
    weight = resid[...] * gains
    near = jnp.zeros((TAPS, groups), F32)
    far = jnp.zeros((TAPS, groups), F32)
    for n in range(poles):
        term = weight[n : n + 1] * jnp.exp(-rates[n : n + 1] * lag)
        near = near + term
        far = far + term * jnp.exp(-rates[n : n + 1] * float(TAPS))
    taps_out[0] = dot_t(near.astype(BF16), turn)
    taps_out[1] = dot_t(far.astype(BF16), turn)
    for tile in range(width // LANES):
        at = pl.ds(tile * LANES, LANES)
        wide = spread(rates[...], tile * (LANES // size), size, LANES)
        rates_out[:, at] = wide
        gains_out[:, at] = gain(wide)


def states_kernel(
    cap,
    size,
    events,
    halo,
    value,
    key,
    rows,
    masks,
    rates,
    gains,
    mixed_out,
    ends_out,
    wide,
    state,
):
    poles, width = rates.shape
    length, block = value.shape
    peers = ends_out.shape[0]
    step = pl.program_id(0)
    per_tile = LANES // size
    part = state.shape[1]

    for tile in range(block // LANES):
        at = slice(tile * LANES, (tile + 1) * LANES)
        spot = pl.ds(pl.multiple_of(step * block + tile * LANES, LANES), LANES)
        x = value[:, at]
        window = jnp.concatenate([halo[:, at], x[:TAPS]], axis=0)
        blocks = [
            circulant(rows[tile * per_tile + g : tile * per_tile + g + 1]) for g in range(per_tile)
        ]
        mixed0 = filtered(blocks, masks, 0, 1, window, key[:TAPS, at])
        mixed1 = filtered(blocks, masks, 2, 3, x, key[TAPS:, at])
        mixed_out[:TAPS, at] = mixed0
        mixed_out[TAPS:, at] = mixed1
        wide[:TAPS, spot] = mixed0.astype(F32)
        wide[TAPS:, spot] = mixed1.astype(F32)

    @pl.when(step == pl.num_programs(0) - 1)
    def recur():
        ends_out[...] = jnp.zeros(ends_out.shape, BF16)
        for h in range(width // part):
            lanes = pl.ds(h * part, part)
            fade = jnp.exp(-rates[:, lanes])
            state[...] = jnp.zeros((poles, part), F32)

            def run(c, carry):
                base = pl.multiple_of(c * CHUNK, CHUNK)
                event = events[length + c] != 0

                @pl.when(jnp.logical_not(event))
                def plain():
                    s = state[...]
                    for t in range(CHUNK):
                        s = fade * s + wide[pl.ds(base + t, 1), lanes]
                    state[...] = s

                @pl.when(event)
                def marked():
                    s = state[...]
                    for t in range(CHUNK):
                        code = events[base + t]
                        s = jnp.where((code & 1) != 0, 0.0, s)
                        s = fade * s + wide[pl.ds(base + t, 1), lanes]

                        @pl.when(code >= 2)
                        def keep(s=s, code=code):
                            row = code // 2 - 1
                            ends_out[row // cap, lax.rem(row, cap), :, lanes] = (
                                s * gains[:, lanes]
                            ).astype(BF16)

                    state[...] = s

                return carry

            lax.fori_loop(0, length // CHUNK, run, 0)
            through = (state[...] * gains[:, lanes]).astype(BF16)
            for r in range(peers):
                ends_out[r, cap, :, lanes] = through


def local_kernel(
    size, offsets, place, mixed, masks, taps, skip, rates, resid, local_out, high_out, low_out, limit
):
    length, block = mixed.shape
    begin = place[0] * length
    step = pl.program_id(0)
    per_tile = LANES // size

    @pl.when(step == 0)
    def prepare():
        doc = doc_at(offsets, begin)
        limit[0] = jnp.where(offsets[doc] < begin, offsets[doc + 1] - begin, 0)

    t = iota((length, LANES), 0)
    lane_group = iota((TAPS, LANES), 1) // size
    for tile in range(block // LANES):
        at = slice(tile * LANES, (tile + 1) * LANES)
        x = mixed[:, at]
        acc0 = jnp.zeros((TAPS, LANES), F32)
        acc1 = jnp.zeros((TAPS, LANES), F32)
        for g in range(per_tile):
            row = tile * per_tile + g
            a, b = circulant(taps[0, row : row + 1]), circulant(taps[1, row : row + 1])
            y0 = dot(a * masks[1], x[:TAPS])
            y1 = dot(jnp.concatenate([a * masks[2] + b * masks[4], a * masks[3]], axis=1), x)
            acc0 = jnp.where(lane_group == g, y0, acc0)
            acc1 = jnp.where(lane_group == g, y1, acc1)
        local_out[:, at] = jnp.concatenate([acc0, acc1], axis=0) + skip[:, at] * x.astype(F32)
        weight = jnp.exp(-rates[:, at] * (t + 1).astype(F32)) * resid[:, at]
        weight = jnp.where(t < limit[0], weight, 0.0)
        high = weight.astype(BF16)
        high_out[:, at] = high
        low_out[:, at] = (weight - high.astype(F32)).astype(BF16)


def slots_kernel(length, offsets, owners, place, got, rates, after, slot_out, entering_out):
    peers, cap = got.shape[0], got.shape[1] - 1
    slots = slot_out.shape[0]
    me = place[0]
    p = rates[...]
    fade = jnp.exp(-p * float(length))

    def entering(first, stop):
        def hop(c, state):
            return fade * state + got[c, cap].astype(F32)

        return lax.fori_loop(first, stop, hop, jnp.zeros(p.shape, F32))

    my_start = offsets[doc_at(offsets, me * length)]
    entering_out[...] = entering(my_start // length, me)
    for k in range(slots):
        doc = owners[me * slots + k]
        start, end = offsets[doc], offsets[doc + 1] - 1
        source = end // length
        link = jnp.exp(-p * (end - source * length + 1).astype(F32))
        state = got[source, k % cap].astype(F32) + link * entering(start // length, source)
        slot_out[k] = state.astype(BF16)


def output_kernel(size, query, local, entering, w_high, w_low, out):
    poles, width = entering.shape
    tile = 2 * LANES
    kept = iota((tile, tile), 0) // poles == iota((tile, tile), 1) // size
    kept = kept.astype(F32).astype(BF16)
    for first in range(0, width, tile):
        at = slice(first, first + tile)
        e = entering[:, at]
        e_high = e.astype(BF16)
        e_low = (e - e_high.astype(F32)).astype(BF16)
        b_high = jnp.concatenate([e_high] * (tile // size), axis=0) * kept
        b_low = jnp.concatenate([e_low] * (tile // size), axis=0) * kept
        fix = dot(w_high[:, at], b_high) + dot(w_low[:, at], b_high) + dot(w_high[:, at], b_low)
        out[:, at] = (query[:, at].astype(F32) * (local[:, at] + fix)).astype(BF16)


def widen_kernel(x, out):
    out[...] = x[...].astype(F32)


def per_device(query, key, value, filt, rates, resid, skip, offsets, owners):
    length, width = value.shape
    poles, groups = rates.shape
    size = width // groups
    peers, lines = lax.axis_size("ctx"), lax.axis_size("ch")
    slots = owners.shape[0] // peers
    cap = -(-ENDS // peers)
    place = lax.axis_index("ctx").astype(jnp.int32).reshape(1)
    rates_flat = rates.T.reshape(1, groups * poles)
    resid_flat = resid.T.reshape(1, groups * poles)

    halo = lax.ppermute(
        value[length - TAPS :], "ctx", [(i, i + 1) for i in range(peers - 1)]
    )

    def whole(shape):
        return pl.BlockSpec(shape, lambda i: (0,) * len(shape))

    block = min(width, BLOCK)

    def lanes(height):
        return pl.BlockSpec((height, block), lambda i: (0, i))

    vmem = pl.BlockSpec(memory_space=pltpu.VMEM)
    rates_wide, gains_wide, rows, masks, taps, events = pl.pallas_call(
        functools.partial(prepare_kernel, cap, peers, size),
        in_specs=[SMEM] * 3 + [vmem] * 3,
        out_specs=[vmem] * 5 + [SMEM],
        out_shape=[
            jax.ShapeDtypeStruct((poles, width), F32),
            jax.ShapeDtypeStruct((poles, width), F32),
            jax.ShapeDtypeStruct((groups, TAPS), F32),
            jax.ShapeDtypeStruct((5, TAPS, TAPS), BF16),
            jax.ShapeDtypeStruct((2, groups, TAPS), F32),
            jax.ShapeDtypeStruct((length + length // CHUNK,), jnp.int32),
        ],
        compiler_params=params(0),
        cost_estimate=pl.CostEstimate(flops=1 << 30, bytes_accessed=1 << 20, transcendentals=0),
        name="prepare",
    )(offsets, owners, place, filt, rates, resid)

    part = min(width, PART)
    mixed, ends = pl.pallas_call(
        functools.partial(states_kernel, cap, size),
        grid=(width // block,),
        in_specs=[
            SMEM,
            lanes(TAPS),
            lanes(length),
            lanes(length),
            pl.BlockSpec((block // size, TAPS), lambda i: (i, 0)),
            whole((5, TAPS, TAPS)),
            whole((poles, width)),
            whole((poles, width)),
        ],
        out_specs=[lanes(length), whole((peers, cap + 1, poles, width))],
        out_shape=[
            jax.ShapeDtypeStruct((length, width), BF16),
            jax.ShapeDtypeStruct((peers, cap + 1, poles, width), BF16),
        ],
        scratch_shapes=[pltpu.VMEM((length, width), F32), pltpu.VMEM((poles, part), F32)],
        compiler_params=params(1),
        name="states",
    )(events, halo, value, key, rows, masks, rates_wide, gains_wide)

    got = lax.all_to_all(ends, "ctx", split_axis=0, concat_axis=0, tiled=True)

    local, w_high, w_low = pl.pallas_call(
        functools.partial(local_kernel, size),
        grid=(width // block,),
        in_specs=[
            SMEM,
            SMEM,
            lanes(length),
            whole((5, TAPS, TAPS)),
            pl.BlockSpec((2, block // size, TAPS), lambda i: (0, i, 0)),
            lanes(1),
            lanes(1),
            lanes(1),
        ],
        out_specs=[lanes(length)] * 3,
        out_shape=[
            jax.ShapeDtypeStruct((length, width), F32),
            jax.ShapeDtypeStruct((length, width), BF16),
            jax.ShapeDtypeStruct((length, width), BF16),
        ],
        scratch_shapes=[pltpu.SMEM((1,), jnp.int32)],
        compiler_params=params(1),
        cost_estimate=pl.CostEstimate(
            flops=32 * length * length * width, bytes_accessed=6 * length * width, transcendentals=0
        ),
        name="local",
    )(offsets, place, mixed, masks, taps, skip.reshape(1, width), rates_flat, resid_flat)

    picked, entering = pl.pallas_call(
        functools.partial(slots_kernel, length),
        in_specs=[SMEM, SMEM, SMEM, vmem, vmem, pl.BlockSpec(memory_space=pl.ANY)],
        out_specs=[vmem] * 2,
        out_shape=[
            jax.ShapeDtypeStruct((slots, poles, width), BF16),
            jax.ShapeDtypeStruct((poles, width), F32),
        ],
        compiler_params=params(0),
        name="slots",
    )(offsets, owners, place, got, rates_wide, local)

    gathered = lax.all_to_all(picked, "ch", split_axis=0, concat_axis=0, tiled=True)

    output = pl.pallas_call(
        functools.partial(output_kernel, size),
        grid=(width // block,),
        in_specs=[lanes(length), lanes(length), lanes(poles), lanes(length), lanes(length)],
        out_specs=lanes(length),
        out_shape=jax.ShapeDtypeStruct((length, width), BF16),
        compiler_params=params(1),
        cost_estimate=pl.CostEstimate(
            flops=3 * 512 * length * width, bytes_accessed=12 * length * width, transcendentals=0
        ),
        name="output",
    )(query, local, entering, w_high, w_low)

    per_line = slots // lines
    doc_states = pl.pallas_call(
        widen_kernel,
        grid=(lines,),
        in_specs=[pl.BlockSpec((per_line, poles, width), lambda h: (h, 0, 0))],
        out_specs=pl.BlockSpec((per_line, poles, width), lambda h: (0, 0, h)),
        out_shape=jax.ShapeDtypeStruct((per_line, poles, lines * width), F32),
        compiler_params=params(1),
        name="widen",
    )(gathered)
    return (output, doc_states)


def solution(mesh):
    placed = (
        P("ctx", "ch"),
        P("ctx", "ch"),
        P("ctx", "ch"),
        P(None, "ch"),
        P(None, "ch"),
        P(None, "ch"),
        P("ch"),
        P(),
        P(),
    )
    return jax.shard_map(
        per_device,
        mesh=mesh,
        in_specs=placed,
        out_specs=(P("ctx", "ch"), P(("ctx", "ch"), None, None)),
        check_vma=False,
    )
```

```python
import functools

import jax
import jax.numpy as jnp
from jax import lax
from jax.experimental import pallas as pl
from jax.experimental.pallas import tpu as pltpu
from jax.sharding import PartitionSpec as P

TAPS = 128
ENDS = 16
LANES = 128
BLOCK = 512
CHUNK = 16
F32 = jnp.float32
BF16 = jnp.bfloat16

SMEM = pl.BlockSpec(memory_space=pltpu.SMEM)


def params(grid_dims, mebibytes):
    return pltpu.CompilerParams(
        dimension_semantics=("arbitrary",) * grid_dims, vmem_limit_bytes=mebibytes * 1024 * 1024
    )


def iota(shape, dim):
    return lax.broadcasted_iota(jnp.int32, shape, dim)


def dot(a, b):
    return lax.dot_general(a, b, (((1,), (0,)), ((), ())), preferred_element_type=F32)


def dot_t(a, b):
    return lax.dot_general(a, b, (((0,), (0,)), ((), ())), preferred_element_type=F32)


def spread(x, first_group, size, lanes):
    groups = x.shape[1]
    pick = (iota((groups, lanes), 0) == first_group + iota((groups, lanes), 1) // size).astype(F32)
    pick = pick.astype(BF16)
    high = x.astype(BF16)
    rest = x - high.astype(F32)
    mid = rest.astype(BF16)
    low = (rest - mid.astype(F32)).astype(BF16)
    return dot(high, pick) + dot(mid, pick) + dot(low, pick)


def gain(rates):
    x = 2.0 * rates
    tail = 1.0 - x / 9.0
    for k in range(8, 1, -1):
        tail = 1.0 - x * tail * (1.0 / k)
    return jnp.sqrt(x * tail)


def circulant(row):
    return pltpu.roll(
        jnp.broadcast_to(row, (TAPS, TAPS)), 0, 1, stride=1, stride_axis=0
    ).astype(BF16)


def doc_at(offsets, position):
    docs = offsets.shape[0] - 1
    low, high = jnp.int32(0), jnp.int32(docs)
    for _ in range(docs.bit_length()):
        middle = (low + high) // 2
        left = offsets[middle] <= position
        low, high = jnp.where(left, middle, low), jnp.where(left, high, middle)
    return low


def filtered(blocks, masks, earlier, current, window, key):
    lane_group = iota((TAPS, LANES), 1) // (LANES // len(blocks))
    total = jnp.zeros((TAPS, LANES), F32)
    for g, c in enumerate(blocks):
        y = dot(jnp.concatenate([c * masks[earlier], c * masks[current]], axis=1), window)
        total = jnp.where(lane_group == g, y, total)
    return (key.astype(F32) * total).astype(BF16)


def prepare_kernel(
    cap,
    peers,
    size,
    offsets,
    owners,
    place,
    filt,
    rates,
    resid,
    rates_out,
    gains_out,
    rows_out,
    masks_out,
    taps_out,
    keep,
    last,
):
    poles, groups = rates.shape
    width = rates_out.shape[1]
    length = 2 * TAPS
    docs = offsets.shape[0] - 1
    chosen = owners.shape[0]
    begin = place[0] * length
    d0 = doc_at(offsets, begin)

    def clear(t, carry):
        for u in range(8):
            keep[t * 8 + u] = jnp.float32(1.0)
        return carry

    lax.fori_loop(0, length // 8, clear, 0)
    for row in range(peers * cap):
        last[row] = 0

    def mark(k, carry):
        doc = d0 + k
        order = lax.rem(doc - owners[0] + docs, docs)
        start = offsets[jnp.minimum(doc, docs)] - begin
        end = offsets[jnp.minimum(doc + 1, docs)] - 1 - begin

        @pl.when((doc < docs) & (start >= 0) & (start < length))
        def opens():
            keep[start] = jnp.float32(0.0)

        @pl.when((doc < docs) & (end < length) & (order < chosen))
        def closes():
            last[lax.rem(order, peers) * cap + lax.rem(order // peers, cap)] = end

        return carry

    lax.fori_loop(0, ENDS + 1, mark, 0)

    spot = begin + iota((length, LANES), 0)
    starts = jnp.broadcast_to(offsets[d0], (length, LANES))
    for k in range(1, ENDS + 1):
        off = offsets[jnp.minimum(d0 + k, docs)]
        starts = jnp.where(spot >= off, off, starts)
    i, j = iota((TAPS, TAPS), 0), iota((TAPS, TAPS), 1)
    s0, s1 = starts[:TAPS], starts[TAPS:]
    cross = s1 <= begin + j
    for index, mask in enumerate(
        (
            (j > i) & (s0 <= begin - TAPS + j),
            (j <= i) & (s0 <= begin + j),
            (j > i) & cross,
            (j <= i) & (s1 <= begin + TAPS + j),
            (j <= i) & cross,
        )
    ):
        masks_out[index] = mask.astype(F32).astype(BF16)
    turn = (i == (TAPS - j) % TAPS).astype(F32).astype(BF16)
    rows_out[...] = dot_t(filt[...], turn)
    lag = iota((TAPS, groups), 0).astype(F32)
    gains = gain(rates[...])
    weight = resid[...] * gains
    near = jnp.zeros((TAPS, groups), F32)
    far = jnp.zeros((TAPS, groups), F32)
    for n in range(poles):
        term = weight[n : n + 1] * jnp.exp(-rates[n : n + 1] * lag)
        near = near + term
        far = far + term * jnp.exp(-rates[n : n + 1] * float(TAPS))
    taps_out[0] = dot_t(near.astype(BF16), turn)
    taps_out[1] = dot_t(far.astype(BF16), turn)
    for tile in range(width // LANES):
        at = pl.ds(tile * LANES, LANES)
        wide = spread(rates[...], tile * (LANES // size), size, LANES)
        rates_out[:, at] = wide
        gains_out[:, at] = gain(wide)


def states_kernel(
    cap,
    size,
    place,
    keep,
    last,
    halo,
    value,
    key,
    rows,
    masks,
    rates,
    gains,
    mixed_out,
    *rest,
):
    ends_out, (wide, history) = rest[:-2], rest[-2:]
    poles, width = rates.shape
    length, block = value.shape
    peers = len(ends_out)
    step = pl.program_id(0)
    per_tile = LANES // size

    for tile in range(block // LANES):
        at = slice(tile * LANES, (tile + 1) * LANES)
        spot = pl.ds(pl.multiple_of(step * block + tile * LANES, LANES), LANES)
        x = value[:, at]
        window = jnp.concatenate([halo[:, at], x[:TAPS]], axis=0)
        blocks = [
            circulant(rows[tile * per_tile + g : tile * per_tile + g + 1]) for g in range(per_tile)
        ]
        mixed0 = filtered(blocks, masks, 0, 1, window, key[:TAPS, at])
        mixed1 = filtered(blocks, masks, 2, 3, x, key[TAPS:, at])
        mixed_out[:TAPS, at] = mixed0
        mixed_out[TAPS:, at] = mixed1
        wide[:TAPS, spot] = mixed0.astype(F32)
        wide[TAPS:, spot] = mixed1.astype(F32)

    @pl.when(step == pl.num_programs(0) - 1)
    def run():
        for first in range(0, width, block):
            lanes = slice(first, first + block)
            fade = jnp.exp(-rates[:, lanes])

            def some(c, state):
                base = pl.multiple_of(c * CHUNK, CHUNK)
                for t in range(CHUNK):
                    state = (fade * keep[base + t]) * state + wide[pl.ds(base + t, 1), lanes]
                    history[base + t] = state
                return state

            state = lax.fori_loop(0, length // CHUNK, some, jnp.zeros((poles, block), F32))
            scale = gains[:, lanes]
            through = (state * scale).astype(BF16)
            for d in range(peers):
                peer = lax.rem(place[0] + d, peers)
                for i in range(cap):
                    end = history[last[peer * cap + i]]
                    ends_out[d][i, :, lanes] = (end * scale).astype(BF16)
                ends_out[d][cap, :, lanes] = through


def local_kernel(
    size, offsets, place, mixed, masks, taps, skip, rates, resid, local_out, weight_out, limit
):
    length, block = mixed.shape
    begin = place[0] * length
    step = pl.program_id(0)
    per_tile = LANES // size

    @pl.when(step == 0)
    def prepare():
        doc = doc_at(offsets, begin)
        limit[0] = jnp.where(offsets[doc] < begin, offsets[doc + 1] - begin, 0)

    t = iota((length, LANES), 0)
    lane_group = iota((TAPS, LANES), 1) // size
    for tile in range(block // LANES):
        at = slice(tile * LANES, (tile + 1) * LANES)
        x = mixed[:, at]
        acc0 = jnp.zeros((TAPS, LANES), F32)
        acc1 = jnp.zeros((TAPS, LANES), F32)
        for g in range(per_tile):
            row = tile * per_tile + g
            a, b = circulant(taps[0, row : row + 1]), circulant(taps[1, row : row + 1])
            y0 = dot(a * masks[1], x[:TAPS])
            y1 = dot(jnp.concatenate([a * masks[2] + b * masks[4], a * masks[3]], axis=1), x)
            acc0 = jnp.where(lane_group == g, y0, acc0)
            acc1 = jnp.where(lane_group == g, y1, acc1)
        local_out[:, at] = jnp.concatenate([acc0, acc1], axis=0) + skip[:, at] * x.astype(F32)
        weight = jnp.exp(-rates[:, at] * (t + 1).astype(F32)) * resid[:, at]
        weight = jnp.where(t < limit[0], weight, 0.0)
        weight_out[:, at] = weight.astype(BF16)


def slots_kernel(length, lines, peers, offsets, owners, place, line, *rest):
    got, (rates, after, entering_out) = rest[:peers], rest[peers : peers + 3]
    slot_outs = rest[peers + 3 : peers + 3 + lines]
    through, mine, sems = rest[peers + 3 + lines :]
    cap = got[0].shape[0] - 1
    per_line = slot_outs[0].shape[0]
    me = place[0]
    arriving = []
    for d in range(peers):
        source = lax.rem(me - d + peers, peers)
        arriving.append(pltpu.make_async_copy(got[d].at[cap], through.at[source], sems.at[d]))
        arriving[-1].start()
    spans = []
    for d in range(lines):
        for q in range(per_line):
            k = lax.rem(line[0] + d, lines) * per_line + q
            doc = owners[me * (lines * per_line) + k]
            start, end = offsets[doc], offsets[doc + 1] - 1
            spot = d * per_line + q
            behind = lax.rem(me - end // length + peers, peers)
            for e in range(peers):

                @pl.when(behind == e)
                def fetch(e=e, k=k, spot=spot):
                    pltpu.make_async_copy(
                        got[e].at[lax.rem(k, cap)], mine.at[spot], sems.at[peers + spot]
                    ).start()

            spans.append((start, end))
    p = rates[...]
    fade = jnp.exp(-p * float(length))

    def entering(first, stop):
        def hop(c, state):
            return fade * state + through[c].astype(F32)

        return lax.fori_loop(first, stop, hop, jnp.zeros(p.shape, F32))

    my_start = offsets[doc_at(offsets, me * length)]
    for copy in arriving:
        copy.wait()
    for spot, (start, end) in enumerate(spans):
        source = end // length
        link = jnp.exp(-p * (end - source * length + 1).astype(F32))
        extra = link * entering(start // length, source)
        pltpu.make_async_copy(got[0].at[0], mine.at[spot], sems.at[peers + spot]).wait()
        state = mine[spot].astype(F32) + extra
        slot_outs[spot // per_line][spot % per_line] = state.astype(BF16)
    entering_out[...] = entering(my_start // length, me)


def output_kernel(size, query, local, entering, weight, out):
    poles, width = entering.shape
    tile = 2 * LANES
    kept = iota((tile, tile), 0) // poles == iota((tile, tile), 1) // size
    kept = kept.astype(F32).astype(BF16)
    for first in range(0, width, tile):
        at = slice(first, first + tile)
        spread_out = jnp.concatenate([entering[:, at].astype(BF16)] * (tile // size), axis=0) * kept
        fix = dot(weight[:, at], spread_out)
        out[:, at] = (query[:, at].astype(F32) * (local[:, at] + fix)).astype(BF16)


def widen_kernel(line, *refs):
    parts, out = refs[:-1], refs[-1]
    width = parts[0].shape[2]
    for d, part in enumerate(parts):
        source = lax.rem(line[0] - d + len(parts), len(parts))
        out[:, :, pl.ds(pl.multiple_of(source * width, width), width)] = part[...].astype(F32)


def per_device(query, key, value, filt, rates, resid, skip, offsets, owners):
    length, width = value.shape
    poles, groups = rates.shape
    size = width // groups
    peers, lines = lax.axis_size("ctx"), lax.axis_size("ch")
    slots = owners.shape[0] // peers
    cap = -(-ENDS // peers)
    line = lax.axis_index("ch").astype(jnp.int32).reshape(1)
    place = lax.axis_index("ctx").astype(jnp.int32).reshape(1)
    rates_flat = rates.T.reshape(1, groups * poles)
    resid_flat = resid.T.reshape(1, groups * poles)

    halo = lax.ppermute(
        value[length - TAPS :], "ctx", [(i, i + 1) for i in range(peers - 1)]
    )

    def whole(shape):
        return pl.BlockSpec(shape, lambda i: (0,) * len(shape))

    block = min(width, BLOCK)

    def lanes(height):
        return pl.BlockSpec((height, block), lambda i: (0, i))

    vmem = pl.BlockSpec(memory_space=pltpu.VMEM)
    hbm = pl.BlockSpec(memory_space=pl.ANY)
    rates_wide, gains_wide, rows, masks, taps, keep, last = pl.pallas_call(
        functools.partial(prepare_kernel, cap, peers, size),
        in_specs=[SMEM] * 3 + [vmem] * 3,
        out_specs=[vmem] * 5 + [SMEM] * 2,
        out_shape=[
            jax.ShapeDtypeStruct((poles, width), F32),
            jax.ShapeDtypeStruct((poles, width), F32),
            jax.ShapeDtypeStruct((groups, TAPS), F32),
            jax.ShapeDtypeStruct((5, TAPS, TAPS), BF16),
            jax.ShapeDtypeStruct((2, groups, TAPS), F32),
            jax.ShapeDtypeStruct((length,), F32),
            jax.ShapeDtypeStruct((peers * cap,), jnp.int32),
        ],
        compiler_params=params(0, 60),
        cost_estimate=pl.CostEstimate(flops=1 << 30, bytes_accessed=1 << 20, transcendentals=0),
        name="prepare",
    )(offsets, owners, place, filt, rates, resid)

    mixed, *ends = pl.pallas_call(
        functools.partial(states_kernel, cap, size),
        grid=(width // block,),
        in_specs=[
            SMEM,
            SMEM,
            SMEM,
            lanes(TAPS),
            lanes(length),
            lanes(length),
            pl.BlockSpec((block // size, TAPS), lambda i: (i, 0)),
            whole((5, TAPS, TAPS)),
            whole((poles, width)),
            whole((poles, width)),
        ],
        out_specs=[lanes(length)] + [whole((cap + 1, poles, width))] * peers,
        out_shape=[jax.ShapeDtypeStruct((length, width), BF16)]
        + [jax.ShapeDtypeStruct((cap + 1, poles, width), BF16)] * peers,
        scratch_shapes=[
            pltpu.VMEM((length, width), F32),
            pltpu.VMEM((length, poles, block), F32),
        ],
        compiler_params=params(1, 56),
        name="states",
    )(place, keep, last, halo, value, key, rows, masks, rates_wide, gains_wide)

    got = [ends[0]]
    for d in range(1, peers):
        route = [(i, (i + d) % peers) for i in range(peers)]
        got.append(lax.ppermute(ends[d], "ctx", route))

    local, weight = pl.pallas_call(
        functools.partial(local_kernel, size),
        grid=(width // block,),
        in_specs=[
            SMEM,
            SMEM,
            lanes(length),
            whole((5, TAPS, TAPS)),
            pl.BlockSpec((2, block // size, TAPS), lambda i: (0, i, 0)),
            lanes(1),
            lanes(1),
            lanes(1),
        ],
        out_specs=[lanes(length)] * 2,
        out_shape=[
            jax.ShapeDtypeStruct((length, width), F32),
            jax.ShapeDtypeStruct((length, width), BF16),
        ],
        scratch_shapes=[pltpu.SMEM((1,), jnp.int32)],
        compiler_params=params(1, 48),
        cost_estimate=pl.CostEstimate(
            flops=32 * length * length * width, bytes_accessed=6 * length * width, transcendentals=0
        ),
        name="local",
    )(offsets, place, mixed, masks, taps, skip.reshape(1, width), rates_flat, resid_flat)

    per_line = slots // lines
    entering, *picked = pl.pallas_call(
        functools.partial(slots_kernel, length, lines, peers),
        in_specs=[SMEM] * 4 + [hbm] * peers + [vmem, hbm],
        out_specs=[vmem] * (1 + lines),
        out_shape=[jax.ShapeDtypeStruct((poles, width), F32)]
        + [jax.ShapeDtypeStruct((per_line, poles, width), BF16)] * lines,
        scratch_shapes=[
            pltpu.VMEM((peers, poles, width), BF16),
            pltpu.VMEM((slots, poles, width), BF16),
            pltpu.SemaphoreType.DMA((peers + slots,)),
        ],
        compiler_params=params(0, 16),
        name="slots",
    )(offsets, owners, place, line, *got, rates_wide, local)

    arrived = [picked[0]]
    for d in range(1, lines):
        route = [(i, (i + d) % lines) for i in range(lines)]
        arrived.append(lax.ppermute(picked[d], "ch", route))

    output = pl.pallas_call(
        functools.partial(output_kernel, size),
        grid=(width // block,),
        in_specs=[lanes(length), lanes(length), lanes(poles), lanes(length)],
        out_specs=lanes(length),
        out_shape=jax.ShapeDtypeStruct((length, width), BF16),
        compiler_params=params(1, 60),
        cost_estimate=pl.CostEstimate(
            flops=3 * 512 * length * width, bytes_accessed=12 * length * width, transcendentals=0
        ),
        name="output",
    )(query, local, entering, weight)

    doc_states = pl.pallas_call(
        widen_kernel,
        in_specs=[SMEM] + [vmem] * lines,
        out_specs=vmem,
        out_shape=jax.ShapeDtypeStruct((per_line, poles, lines * width), F32),
        compiler_params=params(0, 16),
        name="widen",
    )(line, *arrived)
    return (output, doc_states)


def solution(mesh):
    placed = (
        P("ctx", "ch"),
        P("ctx", "ch"),
        P("ctx", "ch"),
        P(None, "ch"),
        P(None, "ch"),
        P(None, "ch"),
        P("ch"),
        P(),
        P(),
    )
    return jax.shard_map(
        per_device,
        mesh=mesh,
        in_specs=placed,
        out_specs=(P("ctx", "ch"), P(("ctx", "ch"), None, None)),
        check_vma=False,
    )
```

```python
import functools

import jax
import jax.numpy as jnp
from jax import lax
from jax.experimental import pallas as pl
from jax.experimental.pallas import tpu as pltpu
from jax.sharding import PartitionSpec as P

TAPS = 128
ENDS = 16
LANES = 128
BLOCK = 512
CHUNK = 16
F32 = jnp.float32
BF16 = jnp.bfloat16

SMEM = pl.BlockSpec(memory_space=pltpu.SMEM)


def params(grid_dims, mebibytes):
    return pltpu.CompilerParams(
        dimension_semantics=("arbitrary",) * grid_dims, vmem_limit_bytes=mebibytes * 1024 * 1024
    )


def iota(shape, dim):
    return lax.broadcasted_iota(jnp.int32, shape, dim)


def dot(a, b):
    return lax.dot_general(a, b, (((1,), (0,)), ((), ())), preferred_element_type=F32)


def dot_t(a, b):
    return lax.dot_general(a, b, (((0,), (0,)), ((), ())), preferred_element_type=F32)


def spread(x, first_group, size, lanes):
    groups = x.shape[1]
    pick = (iota((groups, lanes), 0) == first_group + iota((groups, lanes), 1) // size).astype(F32)
    pick = pick.astype(BF16)
    high = x.astype(BF16)
    rest = x - high.astype(F32)
    mid = rest.astype(BF16)
    low = (rest - mid.astype(F32)).astype(BF16)
    return dot(high, pick) + dot(mid, pick) + dot(low, pick)


def gain(rates):
    x = 2.0 * rates
    tail = 1.0 - x / 9.0
    for k in range(8, 1, -1):
        tail = 1.0 - x * tail * (1.0 / k)
    return jnp.sqrt(x * tail)


def circulant(row):
    return pltpu.roll(
        jnp.broadcast_to(row, (TAPS, TAPS)), 0, 1, stride=1, stride_axis=0
    ).astype(BF16)


def doc_at(offsets, position):
    docs = offsets.shape[0] - 1
    low, high = jnp.int32(0), jnp.int32(docs)
    for _ in range(docs.bit_length()):
        middle = (low + high) // 2
        left = offsets[middle] <= position
        low, high = jnp.where(left, middle, low), jnp.where(left, high, middle)
    return low


def filtered(blocks, masks, earlier, current, window, key):
    lane_group = iota((TAPS, LANES), 1) // (LANES // len(blocks))
    total = jnp.zeros((TAPS, LANES), F32)
    for g, c in enumerate(blocks):
        y = dot(jnp.concatenate([c * masks[earlier], c * masks[current]], axis=1), window)
        total = jnp.where(lane_group == g, y, total)
    return (key.astype(F32) * total).astype(BF16)


def prepare_kernel(
    cap,
    peers,
    size,
    offsets,
    owners,
    place,
    filt,
    rates,
    resid,
    rates_out,
    gains_out,
    rows_out,
    masks_out,
    taps_out,
    keep,
    last,
):
    poles, groups = rates.shape
    width = rates_out.shape[1]
    length = 2 * TAPS
    docs = offsets.shape[0] - 1
    chosen = owners.shape[0]
    begin = place[0] * length
    d0 = doc_at(offsets, begin)

    def clear(t, carry):
        for u in range(8):
            keep[t * 8 + u] = jnp.float32(1.0)
        return carry

    lax.fori_loop(0, length // 8, clear, 0)
    for row in range(peers * cap):
        last[row] = 0

    def mark(k, carry):
        doc = d0 + k
        order = doc - owners[0]
        order = jnp.where(order < 0, order + docs, order)
        start = offsets[jnp.minimum(doc, docs)] - begin
        end = offsets[jnp.minimum(doc + 1, docs)] - 1 - begin

        @pl.when((doc < docs) & (start >= 0) & (start < length))
        def opens():
            keep[start] = jnp.float32(0.0)

        @pl.when((doc < docs) & (end < length) & (order < chosen))
        def closes():
            last[lax.rem(order, peers) * cap + lax.rem(order // peers, cap)] = end

        return carry

    lax.fori_loop(0, ENDS + 1, mark, 0)

    spot = begin + iota((length, LANES), 0)
    starts = jnp.broadcast_to(offsets[d0], (length, LANES))
    for k in range(1, ENDS + 1):
        off = offsets[jnp.minimum(d0 + k, docs)]
        starts = jnp.where(spot >= off, off, starts)
    i, j = iota((TAPS, TAPS), 0), iota((TAPS, TAPS), 1)
    s0, s1 = starts[:TAPS], starts[TAPS:]
    cross = s1 <= begin + j
    for index, mask in enumerate(
        (
            (j > i) & (s0 <= begin - TAPS + j),
            (j <= i) & (s0 <= begin + j),
            (j > i) & cross,
            (j <= i) & (s1 <= begin + TAPS + j),
            (j <= i) & cross,
        )
    ):
        masks_out[index] = mask.astype(F32).astype(BF16)
    turn = (i == (TAPS - j) % TAPS).astype(F32).astype(BF16)
    rows_out[...] = dot_t(filt[...], turn)
    lag = iota((TAPS, groups), 0).astype(F32)
    gains = gain(rates[...])
    weight = resid[...] * gains
    near = jnp.zeros((TAPS, groups), F32)
    far = jnp.zeros((TAPS, groups), F32)
    for n in range(poles):
        term = weight[n : n + 1] * jnp.exp(-rates[n : n + 1] * lag)
        near = near + term
        far = far + term * jnp.exp(-rates[n : n + 1] * float(TAPS))
    taps_out[0] = dot_t(near.astype(BF16), turn)
    taps_out[1] = dot_t(far.astype(BF16), turn)
    for tile in range(width // LANES):
        at = pl.ds(tile * LANES, LANES)
        wide = spread(rates[...], tile * (LANES // size), size, LANES)
        rates_out[:, at] = wide
        gains_out[:, at] = gain(wide)


def second_kernel(size, value, key, rows, masks, mixed_out, circulants):
    per_tile = LANES // size
    for tile in range(value.shape[1] // LANES):
        at = slice(tile * LANES, (tile + 1) * LANES)
        blocks = []
        for g in range(tile * per_tile, (tile + 1) * per_tile):
            blocks.append(circulant(rows[g : g + 1]))
            circulants[g] = blocks[-1]
        mixed_out[:, at] = filtered(blocks, masks, 2, 3, value[:, at], key[:, at])


def states_kernel(
    cap,
    size,
    place,
    keep,
    last,
    halo,
    value,
    key,
    circulants,
    masks,
    second,
    rates,
    gains,
    mixed_out,
    *rest,
):
    ends_out, (wide, history) = rest[:-2], rest[-2:]
    poles, width = rates.shape
    length, block = 2 * TAPS, value.shape[1]
    peers = len(ends_out)
    step = pl.program_id(0)
    per_tile = LANES // size

    for tile in range(block // LANES):
        at = slice(tile * LANES, (tile + 1) * LANES)
        spot = pl.ds(pl.multiple_of(step * block + tile * LANES, LANES), LANES)
        window = jnp.concatenate([halo[:, at], value[:, at]], axis=0)
        blocks = [circulants[tile * per_tile + g] for g in range(per_tile)]
        mixed = filtered(blocks, masks, 0, 1, window, key[:, at])
        mixed_out[:, at] = mixed
        wide[:TAPS, spot] = mixed.astype(F32)
        wide[TAPS:, spot] = second[:, at].astype(F32)

    @pl.when(step == pl.num_programs(0) - 1)
    def run():
        for first in range(0, width, block):
            lanes = slice(first, first + block)
            fade = jnp.exp(-rates[:, lanes])

            def some(c, state):
                base = pl.multiple_of(c * CHUNK, CHUNK)
                for t in range(CHUNK):
                    state = (fade * keep[base + t]) * state + wide[pl.ds(base + t, 1), lanes]
                    history[base + t] = state
                return state

            state = lax.fori_loop(0, length // CHUNK, some, jnp.zeros((poles, block), F32))
            scale = gains[:, lanes]
            through = (state * scale).astype(BF16)
            for d in range(peers):
                peer = lax.rem(place[0] + d, peers)
                for i in range(cap):
                    end = history[last[peer * cap + i]]
                    ends_out[d][i, :, lanes] = (end * scale).astype(BF16)
                ends_out[d][cap, :, lanes] = through


def local_kernel(
    size, offsets, place, first, second, masks, taps, skip, rates, resid, local_out, weight_out, limit
):
    length, block = 2 * TAPS, first.shape[1]
    begin = place[0] * length
    step = pl.program_id(0)
    per_tile = LANES // size

    @pl.when(step == 0)
    def prepare():
        doc = doc_at(offsets, begin)
        limit[0] = jnp.where(offsets[doc] < begin, offsets[doc + 1] - begin, 0)

    t = iota((length, LANES), 0)
    lane_group = iota((TAPS, LANES), 1) // size
    for tile in range(block // LANES):
        at = slice(tile * LANES, (tile + 1) * LANES)
        x = jnp.concatenate([first[:, at], second[:, at]], axis=0)
        acc0 = jnp.zeros((TAPS, LANES), F32)
        acc1 = jnp.zeros((TAPS, LANES), F32)
        for g in range(per_tile):
            row = tile * per_tile + g
            a, b = circulant(taps[0, row : row + 1]), circulant(taps[1, row : row + 1])
            y0 = dot(a * masks[1], x[:TAPS])
            y1 = dot(jnp.concatenate([a * masks[2] + b * masks[4], a * masks[3]], axis=1), x)
            acc0 = jnp.where(lane_group == g, y0, acc0)
            acc1 = jnp.where(lane_group == g, y1, acc1)
        total = jnp.concatenate([acc0, acc1], axis=0) + skip[:, at] * x.astype(F32)
        local_out[:, at] = total.astype(BF16)
        weight = jnp.exp(-rates[:, at] * (t + 1).astype(F32)) * resid[:, at]
        weight = jnp.where(t < limit[0], weight, 0.0)
        weight_out[:, at] = weight.astype(BF16)


def slots_kernel(length, lines, peers, offsets, owners, place, line, *rest):
    got, (rates, after, entering_out) = rest[:peers], rest[peers : peers + 3]
    slot_outs = rest[peers + 3 : peers + 3 + lines]
    through, mine, sems = rest[peers + 3 + lines :]
    cap = got[0].shape[0] - 1
    per_line = slot_outs[0].shape[0]
    me = place[0]
    arriving = []
    for d in range(peers):
        source = lax.rem(me - d + peers, peers)
        arriving.append(pltpu.make_async_copy(got[d].at[cap], through.at[source], sems.at[d]))
        arriving[-1].start()
    spans = []
    for d in range(lines):
        for q in range(per_line):
            k = lax.rem(line[0] + d, lines) * per_line + q
            doc = owners[me * (lines * per_line) + k]
            start, end = offsets[doc], offsets[doc + 1] - 1
            spot = d * per_line + q
            behind = lax.rem(me - end // length + peers, peers)
            for e in range(peers):

                @pl.when(behind == e)
                def fetch(e=e, k=k, spot=spot):
                    pltpu.make_async_copy(
                        got[e].at[lax.rem(k, cap)], mine.at[spot], sems.at[peers + spot]
                    ).start()

            spans.append((start, end))
    p = rates[...]
    fade = jnp.exp(-p * float(length))

    def entering(first, stop):
        def hop(c, state):
            return fade * state + through[c].astype(F32)

        return lax.fori_loop(first, stop, hop, jnp.zeros(p.shape, F32))

    my_start = offsets[doc_at(offsets, me * length)]
    for copy in arriving:
        copy.wait()
    for spot, (start, end) in enumerate(spans):
        source = end // length
        link = jnp.exp(-p * (end - source * length + 1).astype(F32))
        extra = link * entering(start // length, source)
        pltpu.make_async_copy(got[0].at[0], mine.at[spot], sems.at[peers + spot]).wait()
        state = mine[spot].astype(F32) + extra
        slot_outs[spot // per_line][spot % per_line] = state.astype(BF16)
    entering_out[...] = entering(my_start // length, me)


def output_kernel(size, query, local, entering, weight, out):
    poles, width = entering.shape
    tile = 2 * LANES
    kept = iota((tile, tile), 0) // poles == iota((tile, tile), 1) // size
    kept = kept.astype(F32).astype(BF16)
    for first in range(0, width, tile):
        at = slice(first, first + tile)
        spread_out = jnp.concatenate([entering[:, at].astype(BF16)] * (tile // size), axis=0) * kept
        fix = dot(weight[:, at], spread_out)
        out[:, at] = (query[:, at].astype(F32) * (local[:, at].astype(F32) + fix)).astype(BF16)


def widen_kernel(line, *refs):
    parts, out = refs[:-1], refs[-1]
    width = parts[0].shape[2]
    for d, part in enumerate(parts):
        source = lax.rem(line[0] - d + len(parts), len(parts))
        out[:, :, pl.ds(pl.multiple_of(source * width, width), width)] = part[...].astype(F32)


def per_device(query, key, value, filt, rates, resid, skip, offsets, owners):
    length, width = value.shape
    poles, groups = rates.shape
    size = width // groups
    peers, lines = lax.axis_size("ctx"), lax.axis_size("ch")
    slots = owners.shape[0] // peers
    cap = -(-ENDS // peers)
    line = lax.axis_index("ch").astype(jnp.int32).reshape(1)
    place = lax.axis_index("ctx").astype(jnp.int32).reshape(1)
    rates_flat = rates.T.reshape(1, groups * poles)
    resid_flat = resid.T.reshape(1, groups * poles)

    halo = lax.ppermute(
        value[length - TAPS :], "ctx", [(i, i + 1) for i in range(peers - 1)]
    )

    def whole(shape):
        return pl.BlockSpec(shape, lambda i: (0,) * len(shape))

    block = min(width, BLOCK)

    def lanes(height, size=block):
        return pl.BlockSpec((height, size), lambda i: (0, i))

    vmem = pl.BlockSpec(memory_space=pltpu.VMEM)
    hbm = pl.BlockSpec(memory_space=pl.ANY)
    rates_wide, gains_wide, rows, masks, taps, keep, last = pl.pallas_call(
        functools.partial(prepare_kernel, cap, peers, size),
        in_specs=[SMEM] * 3 + [vmem] * 3,
        out_specs=[vmem] * 5 + [SMEM] * 2,
        out_shape=[
            jax.ShapeDtypeStruct((poles, width), F32),
            jax.ShapeDtypeStruct((poles, width), F32),
            jax.ShapeDtypeStruct((groups, TAPS), F32),
            jax.ShapeDtypeStruct((5, TAPS, TAPS), BF16),
            jax.ShapeDtypeStruct((2, groups, TAPS), F32),
            jax.ShapeDtypeStruct((length,), F32),
            jax.ShapeDtypeStruct((peers * cap,), jnp.int32),
        ],
        compiler_params=params(0, 60),
        cost_estimate=pl.CostEstimate(flops=1 << 30, bytes_accessed=1 << 20, transcendentals=0),
        name="prepare",
    )(offsets, owners, place, filt, rates, resid)

    def half(row, size=block):
        return pl.BlockSpec((TAPS, size), lambda i: (row, i))

    second, circulants = pl.pallas_call(
        functools.partial(second_kernel, size),
        grid=(width // block,),
        in_specs=[
            lanes(length),
            half(1),
            pl.BlockSpec((block // size, TAPS), lambda i: (i, 0)),
            whole((5, TAPS, TAPS)),
        ],
        out_specs=[half(0), pl.BlockSpec((block // size, TAPS, TAPS), lambda i: (i, 0, 0))],
        out_shape=[
            jax.ShapeDtypeStruct((TAPS, width), BF16),
            jax.ShapeDtypeStruct((groups, TAPS, TAPS), BF16),
        ],
        compiler_params=params(1, 60),
        cost_estimate=pl.CostEstimate(
            flops=16 * length * length * width, bytes_accessed=7 * length * width, transcendentals=0
        ),
        name="second",
    )(value, key, rows, masks)

    first, *ends = pl.pallas_call(
        functools.partial(states_kernel, cap, size),
        grid=(width // block,),
        in_specs=[
            SMEM,
            SMEM,
            SMEM,
            half(0),
            half(0),
            half(0),
            pl.BlockSpec((block // size, TAPS, TAPS), lambda i: (i, 0, 0)),
            whole((5, TAPS, TAPS)),
            half(0),
            whole((poles, width)),
            whole((poles, width)),
        ],
        out_specs=[half(0)] + [whole((cap + 1, poles, width))] * peers,
        out_shape=[jax.ShapeDtypeStruct((TAPS, width), BF16)]
        + [jax.ShapeDtypeStruct((cap + 1, poles, width), BF16)] * peers,
        scratch_shapes=[
            pltpu.VMEM((length, width), F32),
            pltpu.VMEM((length, poles, block), F32),
        ],
        compiler_params=params(1, 50),
        name="states",
    )(place, keep, last, halo, value, key, circulants, masks, second, rates_wide, gains_wide)

    got = [ends[0]]
    for d in range(1, peers):
        route = [(i, (i + d) % peers) for i in range(peers)]
        got.append(lax.ppermute(ends[d], "ctx", route))

    broad = min(width, 8 * LANES)
    local, weight = pl.pallas_call(
        functools.partial(local_kernel, size),
        grid=(width // broad,),
        in_specs=[
            SMEM,
            SMEM,
            half(0, broad),
            half(0, broad),
            whole((5, TAPS, TAPS)),
            pl.BlockSpec((2, broad // size, TAPS), lambda i: (0, i, 0)),
            lanes(1, broad),
            lanes(1, broad),
            lanes(1, broad),
        ],
        out_specs=[lanes(length, broad)] * 2,
        out_shape=[
            jax.ShapeDtypeStruct((length, width), BF16),
            jax.ShapeDtypeStruct((length, width), BF16),
        ],
        scratch_shapes=[pltpu.SMEM((1,), jnp.int32)],
        compiler_params=params(1, 48),
        cost_estimate=pl.CostEstimate(
            flops=32 * length * length * width, bytes_accessed=6 * length * width, transcendentals=0
        ),
        name="local",
    )(offsets, place, first, second, masks, taps, skip.reshape(1, width), rates_flat, resid_flat)

    per_line = slots // lines
    entering, *picked = pl.pallas_call(
        functools.partial(slots_kernel, length, lines, peers),
        in_specs=[SMEM] * 4 + [hbm] * peers + [vmem, hbm],
        out_specs=[vmem] * (1 + lines),
        out_shape=[jax.ShapeDtypeStruct((poles, width), F32)]
        + [jax.ShapeDtypeStruct((per_line, poles, width), BF16)] * lines,
        scratch_shapes=[
            pltpu.VMEM((peers, poles, width), BF16),
            pltpu.VMEM((slots, poles, width), BF16),
            pltpu.SemaphoreType.DMA((peers + slots,)),
        ],
        compiler_params=params(0, 16),
        name="slots",
    )(offsets, owners, place, line, *got, rates_wide, local)

    arrived = [picked[0]]
    for d in range(1, lines):
        route = [(i, (i + d) % lines) for i in range(lines)]
        arrived.append(lax.ppermute(picked[d], "ch", route))

    thin = min(width, 8 * LANES)
    output = pl.pallas_call(
        functools.partial(output_kernel, size),
        grid=(width // thin,),
        in_specs=[lanes(length, thin), lanes(length, thin), lanes(poles, thin), lanes(length, thin)],
        out_specs=lanes(length, thin),
        out_shape=jax.ShapeDtypeStruct((length, width), BF16),
        compiler_params=params(1, 60),
        cost_estimate=pl.CostEstimate(
            flops=3 * 512 * length * width, bytes_accessed=12 * length * width, transcendentals=0
        ),
        name="output",
    )(query, local, entering, weight)

    doc_states = pl.pallas_call(
        widen_kernel,
        in_specs=[SMEM] + [vmem] * lines,
        out_specs=vmem,
        out_shape=jax.ShapeDtypeStruct((per_line, poles, lines * width), F32),
        compiler_params=params(0, 16),
        name="widen",
    )(line, *arrived)
    return (output, doc_states)


def solution(mesh):
    placed = (
        P("ctx", "ch"),
        P("ctx", "ch"),
        P("ctx", "ch"),
        P(None, "ch"),
        P(None, "ch"),
        P(None, "ch"),
        P("ch"),
        P(),
        P(),
    )
    return jax.shard_map(
        per_device,
        mesh=mesh,
        in_specs=placed,
        out_specs=(P("ctx", "ch"), P(("ctx", "ch"), None, None)),
        check_vma=False,
    )
```

```python
import functools

import jax
import jax.numpy as jnp
from jax import lax
from jax.experimental import pallas as pl
from jax.experimental.pallas import tpu as pltpu
from jax.sharding import PartitionSpec as P

TAPS = 128
ENDS = 16
LANES = 128
BLOCK = 1024
PART = 512
CHUNK = 16
F32 = jnp.float32
BF16 = jnp.bfloat16

SMEM = pl.BlockSpec(memory_space=pltpu.SMEM)


def params(grid_dims, mebibytes):
    return pltpu.CompilerParams(
        dimension_semantics=("arbitrary",) * grid_dims, vmem_limit_bytes=mebibytes * 1024 * 1024
    )


def iota(shape, dim):
    return lax.broadcasted_iota(jnp.int32, shape, dim)


def dot(a, b):
    return lax.dot_general(a, b, (((1,), (0,)), ((), ())), preferred_element_type=F32)


def dot_t(a, b):
    return lax.dot_general(a, b, (((0,), (0,)), ((), ())), preferred_element_type=F32)


def spread(x, first_group, size, lanes):
    groups = x.shape[1]
    pick = (iota((groups, lanes), 0) == first_group + iota((groups, lanes), 1) // size).astype(F32)
    pick = pick.astype(BF16)
    high = x.astype(BF16)
    rest = x - high.astype(F32)
    mid = rest.astype(BF16)
    low = (rest - mid.astype(F32)).astype(BF16)
    return dot(high, pick) + dot(mid, pick) + dot(low, pick)


def gain(rates):
    x = 2.0 * rates
    tail = 1.0 - x / 9.0
    for k in range(8, 1, -1):
        tail = 1.0 - x * tail * (1.0 / k)
    return jnp.sqrt(x * tail)


def circulant(row):
    return pltpu.roll(
        jnp.broadcast_to(row, (TAPS, TAPS)), 0, 1, stride=1, stride_axis=0
    ).astype(BF16)


def doc_at(offsets, position):
    docs = offsets.shape[0] - 1
    low, high = jnp.int32(0), jnp.int32(docs)
    for _ in range(docs.bit_length()):
        middle = (low + high) // 2
        left = offsets[middle] <= position
        low, high = jnp.where(left, middle, low), jnp.where(left, high, middle)
    return low


def filtered(blocks, masks, earlier, current, window, key):
    lane_group = iota((TAPS, LANES), 1) // (LANES // len(blocks))
    total = jnp.zeros((TAPS, LANES), F32)
    for g, c in enumerate(blocks):
        y = dot(jnp.concatenate([c * masks[earlier], c * masks[current]], axis=1), window)
        total = jnp.where(lane_group == g, y, total)
    return (key.astype(F32) * total).astype(BF16)


def prepare_kernel(
    cap,
    peers,
    size,
    offsets,
    owners,
    place,
    filt,
    rates,
    resid,
    rates_out,
    gains_out,
    rows_out,
    masks_out,
    taps_out,
    keep,
    last,
):
    poles, groups = rates.shape
    width = rates_out.shape[1]
    length = 2 * TAPS
    docs = offsets.shape[0] - 1
    chosen = owners.shape[0]
    begin = place[0] * length
    d0 = doc_at(offsets, begin)

    def clear(t, carry):
        for u in range(8):
            keep[t * 8 + u] = jnp.float32(1.0)
        return carry

    lax.fori_loop(0, length // 8, clear, 0)
    for row in range(peers * cap):
        last[row] = 0

    def mark(k, carry):
        doc = d0 + k
        order = doc - owners[0]
        order = jnp.where(order < 0, order + docs, order)
        start = offsets[jnp.minimum(doc, docs)] - begin
        end = offsets[jnp.minimum(doc + 1, docs)] - 1 - begin

        @pl.when((doc < docs) & (start >= 0) & (start < length))
        def opens():
            keep[start] = jnp.float32(0.0)

        @pl.when((doc < docs) & (end < length) & (order < chosen))
        def closes():
            last[lax.rem(order, peers) * cap + lax.rem(order // peers, cap)] = end

        return carry

    lax.fori_loop(0, ENDS + 1, mark, 0)

    spot = begin + iota((length, LANES), 0)
    starts = jnp.broadcast_to(offsets[d0], (length, LANES))
    for k in range(1, ENDS + 1):
        off = offsets[jnp.minimum(d0 + k, docs)]
        starts = jnp.where(spot >= off, off, starts)
    i, j = iota((TAPS, TAPS), 0), iota((TAPS, TAPS), 1)
    s0, s1 = starts[:TAPS], starts[TAPS:]
    cross = s1 <= begin + j
    for index, mask in enumerate(
        (
            (j > i) & (s0 <= begin - TAPS + j),
            (j <= i) & (s0 <= begin + j),
            (j > i) & cross,
            (j <= i) & (s1 <= begin + TAPS + j),
            (j <= i) & cross,
        )
    ):
        masks_out[index] = mask.astype(F32).astype(BF16)
    turn = (i == (TAPS - j) % TAPS).astype(F32).astype(BF16)
    rows_out[...] = dot_t(filt[...], turn)
    lag = iota((TAPS, groups), 0).astype(F32)
    gains = gain(rates[...])
    weight = resid[...] * gains
    near = jnp.zeros((TAPS, groups), F32)
    far = jnp.zeros((TAPS, groups), F32)
    for n in range(poles):
        term = weight[n : n + 1] * jnp.exp(-rates[n : n + 1] * lag)
        near = near + term
        far = far + term * jnp.exp(-rates[n : n + 1] * float(TAPS))
    taps_out[0] = dot_t(near.astype(BF16), turn)
    taps_out[1] = dot_t(far.astype(BF16), turn)
    for tile in range(width // LANES):
        at = pl.ds(tile * LANES, LANES)
        wide = spread(rates[...], tile * (LANES // size), size, LANES)
        rates_out[:, at] = wide
        gains_out[:, at] = gain(wide)


def second_kernel(size, value, key, rows, masks, kept):
    per_tile = LANES // size
    tiles = value.shape[1] // LANES
    for tile in range(tiles):
        at = slice(tile * LANES, (tile + 1) * LANES)
        blocks = []
        for g in range(tile * per_tile, (tile + 1) * per_tile):
            blocks.append(circulant(rows[g : g + 1]))
            kept[g] = blocks[-1]
        kept[tiles * per_tile + tile] = filtered(blocks, masks, 2, 3, value[:, at], key[:, at])


def states_kernel(
    cap,
    size,
    place,
    keep,
    last,
    halo,
    value,
    key,
    kept,
    masks,
    rates,
    gains,
    mixed_out,
    *rest,
):
    ends_out, (wide, history) = rest[:-2], rest[-2:]
    poles, width = rates.shape
    length, block = 2 * TAPS, value.shape[1]
    peers = len(ends_out)
    step = pl.program_id(0)
    per_tile = LANES // size

    for tile in range(block // LANES):
        at = slice(tile * LANES, (tile + 1) * LANES)
        spot = pl.ds(pl.multiple_of(step * block + tile * LANES, LANES), LANES)
        window = jnp.concatenate([halo[:, at], value[:, at]], axis=0)
        blocks = [kept[tile * per_tile + g] for g in range(per_tile)]
        second = kept[block // LANES * per_tile + tile]
        mixed = filtered(blocks, masks, 0, 1, window, key[:, at])
        mixed_out[:TAPS, at] = mixed
        mixed_out[TAPS:, at] = second
        wide[:TAPS, spot] = mixed.astype(F32)
        wide[TAPS:, spot] = second.astype(F32)

    @pl.when(step == pl.num_programs(0) - 1)
    def run():
        part = history.shape[2]
        for first in range(0, width, part):
            lanes = slice(first, first + part)
            fade = jnp.exp(-rates[:, lanes])

            def some(c, state):
                base = pl.multiple_of(c * CHUNK, CHUNK)
                for t in range(CHUNK):
                    state = (fade * keep[base + t]) * state + wide[pl.ds(base + t, 1), lanes]
                    history[base + t] = state
                return state

            state = lax.fori_loop(0, length // CHUNK, some, jnp.zeros((poles, part), F32))
            scale = gains[:, lanes]
            through = (state * scale).astype(BF16)
            for d in range(peers):
                peer = lax.rem(place[0] + d, peers)
                for i in range(cap):
                    end = history[last[peer * cap + i]]
                    ends_out[d][i, :, lanes] = (end * scale).astype(BF16)
                ends_out[d][cap, :, lanes] = through


def local_kernel(
    size, offsets, place, mixed, masks, taps, skip, rates, resid, local_out, weight_out, limit
):
    length, block = mixed.shape
    begin = place[0] * length
    step = pl.program_id(0)
    per_tile = LANES // size

    @pl.when(step == 0)
    def prepare():
        doc = doc_at(offsets, begin)
        limit[0] = jnp.where(offsets[doc] < begin, offsets[doc + 1] - begin, 0)

    t = iota((length, LANES), 0)
    lane_group = iota((TAPS, LANES), 1) // size
    for tile in range(block // LANES):
        at = slice(tile * LANES, (tile + 1) * LANES)
        x = mixed[:, at]
        acc0 = jnp.zeros((TAPS, LANES), F32)
        acc1 = jnp.zeros((TAPS, LANES), F32)
        for g in range(per_tile):
            row = tile * per_tile + g
            a, b = circulant(taps[0, row : row + 1]), circulant(taps[1, row : row + 1])
            y0 = dot(a * masks[1], x[:TAPS])
            y1 = dot(jnp.concatenate([a * masks[2] + b * masks[4], a * masks[3]], axis=1), x)
            acc0 = jnp.where(lane_group == g, y0, acc0)
            acc1 = jnp.where(lane_group == g, y1, acc1)
        total = jnp.concatenate([acc0, acc1], axis=0) + skip[:, at] * x.astype(F32)
        local_out[:, at] = total.astype(BF16)
        weight = jnp.exp(-rates[:, at] * (t + 1).astype(F32)) * resid[:, at]
        weight = jnp.where(t < limit[0], weight, 0.0)
        weight_out[:, at] = weight.astype(BF16)


def slots_kernel(length, lines, peers, offsets, owners, place, line, *rest):
    got, (rates, after, entering_out) = rest[:peers], rest[peers : peers + 3]
    slot_outs = rest[peers + 3 : peers + 3 + lines]
    through, mine, sems = rest[peers + 3 + lines :]
    cap = got[0].shape[0] - 1
    per_line = slot_outs[0].shape[0]
    me = place[0]
    arriving = []
    for d in range(peers):
        source = lax.rem(me - d + peers, peers)
        arriving.append(pltpu.make_async_copy(got[d].at[cap], through.at[source], sems.at[d]))
        arriving[-1].start()
    spans = []
    for d in range(lines):
        for q in range(per_line):
            k = (line[0] ^ d) * per_line + q
            doc = owners[me * (lines * per_line) + k]
            start, end = offsets[doc], offsets[doc + 1] - 1
            spot = d * per_line + q
            behind = lax.rem(me - end // length + peers, peers)
            for e in range(peers):

                @pl.when(behind == e)
                def fetch(e=e, k=k, spot=spot):
                    pltpu.make_async_copy(
                        got[e].at[lax.rem(k, cap)], mine.at[spot], sems.at[peers + spot]
                    ).start()

            spans.append((start, end))
    p = rates[...]
    fade = jnp.exp(-p * float(length))

    def entering(first, stop):
        def hop(c, state):
            return fade * state + through[c].astype(F32)

        return lax.fori_loop(first, stop, hop, jnp.zeros(p.shape, F32))

    my_start = offsets[doc_at(offsets, me * length)]
    for copy in arriving:
        copy.wait()
    for spot, (start, end) in enumerate(spans):
        source = end // length
        link = jnp.exp(-p * (end - source * length + 1).astype(F32))
        extra = link * entering(start // length, source)
        pltpu.make_async_copy(got[0].at[0], mine.at[spot], sems.at[peers + spot]).wait()
        state = mine[spot].astype(F32) + extra
        slot_outs[spot // per_line][spot % per_line] = state.astype(BF16)
    entering_out[...] = entering(my_start // length, me)


def output_kernel(size, query, local, entering, weight, out):
    poles, width = entering.shape
    tile = 2 * LANES
    kept = iota((tile, tile), 0) // poles == iota((tile, tile), 1) // size
    kept = kept.astype(F32).astype(BF16)
    for first in range(0, width, tile):
        at = slice(first, first + tile)
        spread_out = jnp.concatenate([entering[:, at].astype(BF16)] * (tile // size), axis=0) * kept
        fix = dot(weight[:, at], spread_out)
        out[:, at] = (query[:, at].astype(F32) * (local[:, at].astype(F32) + fix)).astype(BF16)


def widen_kernel(line, *refs):
    parts, out = refs[:-1], refs[-1]
    width = parts[0].shape[2]
    for d, part in enumerate(parts):
        source = line[0] ^ d
        out[:, :, pl.ds(pl.multiple_of(source * width, width), width)] = part[...].astype(F32)


def per_device(query, key, value, filt, rates, resid, skip, offsets, owners):
    length, width = value.shape
    poles, groups = rates.shape
    size = width // groups
    peers, lines = lax.axis_size("ctx"), lax.axis_size("ch")
    slots = owners.shape[0] // peers
    cap = -(-ENDS // peers)
    line = lax.axis_index("ch").astype(jnp.int32).reshape(1)
    place = lax.axis_index("ctx").astype(jnp.int32).reshape(1)
    rates_flat = rates.T.reshape(1, groups * poles)
    resid_flat = resid.T.reshape(1, groups * poles)

    halo = lax.ppermute(
        value[length - TAPS :], "ctx", [(i, i + 1) for i in range(peers - 1)]
    )

    def whole(shape):
        return pl.BlockSpec(shape, lambda i: (0,) * len(shape))

    block = min(width, BLOCK)

    def lanes(height, size=block):
        return pl.BlockSpec((height, size), lambda i: (0, i))

    vmem = pl.BlockSpec(memory_space=pltpu.VMEM)
    hbm = pl.BlockSpec(memory_space=pl.ANY)
    rates_wide, gains_wide, rows, masks, taps, keep, last = pl.pallas_call(
        functools.partial(prepare_kernel, cap, peers, size),
        in_specs=[SMEM] * 3 + [vmem] * 3,
        out_specs=[vmem] * 5 + [SMEM] * 2,
        out_shape=[
            jax.ShapeDtypeStruct((poles, width), F32),
            jax.ShapeDtypeStruct((poles, width), F32),
            jax.ShapeDtypeStruct((groups, TAPS), F32),
            jax.ShapeDtypeStruct((5, TAPS, TAPS), BF16),
            jax.ShapeDtypeStruct((2, groups, TAPS), F32),
            jax.ShapeDtypeStruct((length,), F32),
            jax.ShapeDtypeStruct((peers * cap,), jnp.int32),
        ],
        compiler_params=params(0, 60),
        cost_estimate=pl.CostEstimate(flops=1 << 30, bytes_accessed=1 << 20, transcendentals=0),
        name="prepare",
    )(offsets, owners, place, filt, rates, resid)

    def half(row, size=block):
        return pl.BlockSpec((TAPS, size), lambda i: (row, i))

    entries = block // size + block // LANES
    kept = pl.pallas_call(
        functools.partial(second_kernel, size),
        grid=(width // block,),
        in_specs=[
            lanes(length),
            half(1),
            pl.BlockSpec((block // size, TAPS), lambda i: (i, 0)),
            whole((5, TAPS, TAPS)),
        ],
        out_specs=pl.BlockSpec((entries, TAPS, TAPS), lambda i: (i, 0, 0)),
        out_shape=jax.ShapeDtypeStruct((width // block * entries, TAPS, TAPS), BF16),
        compiler_params=params(1, 60),
        cost_estimate=pl.CostEstimate(
            flops=16 * length * length * width, bytes_accessed=7 * length * width, transcendentals=0
        ),
        name="second",
    )(value, key, rows, masks)

    mixed, *ends = pl.pallas_call(
        functools.partial(states_kernel, cap, size),
        grid=(width // block,),
        in_specs=[
            SMEM,
            SMEM,
            SMEM,
            half(0),
            half(0),
            half(0),
            pl.BlockSpec((entries, TAPS, TAPS), lambda i: (i, 0, 0)),
            whole((5, TAPS, TAPS)),
            whole((poles, width)),
            whole((poles, width)),
        ],
        out_specs=[lanes(length)] + [whole((cap + 1, poles, width))] * peers,
        out_shape=[jax.ShapeDtypeStruct((length, width), BF16)]
        + [jax.ShapeDtypeStruct((cap + 1, poles, width), BF16)] * peers,
        scratch_shapes=[
            pltpu.VMEM((length, width), F32),
            pltpu.VMEM((length, poles, min(block, PART)), F32),
        ],
        compiler_params=params(1, 50),
        name="states",
    )(place, keep, last, halo, value, key, kept, masks, rates_wide, gains_wide)

    got = [ends[0]]
    for d in range(1, peers):
        route = [(i, (i + d) % peers) for i in range(peers)]
        got.append(lax.ppermute(ends[d], "ctx", route))

    broad = min(width, 8 * LANES)
    local, weight = pl.pallas_call(
        functools.partial(local_kernel, size),
        grid=(width // broad,),
        in_specs=[
            SMEM,
            SMEM,
            lanes(length, broad),
            whole((5, TAPS, TAPS)),
            pl.BlockSpec((2, broad // size, TAPS), lambda i: (0, i, 0)),
            lanes(1, broad),
            lanes(1, broad),
            lanes(1, broad),
        ],
        out_specs=[lanes(length, broad)] * 2,
        out_shape=[
            jax.ShapeDtypeStruct((length, width), BF16),
            jax.ShapeDtypeStruct((length, width), BF16),
        ],
        scratch_shapes=[pltpu.SMEM((1,), jnp.int32)],
        compiler_params=params(1, 48),
        cost_estimate=pl.CostEstimate(
            flops=32 * length * length * width, bytes_accessed=6 * length * width, transcendentals=0
        ),
        name="local",
    )(offsets, place, mixed, masks, taps, skip.reshape(1, width), rates_flat, resid_flat)

    per_line = slots // lines
    entering, *picked = pl.pallas_call(
        functools.partial(slots_kernel, length, lines, peers),
        in_specs=[SMEM] * 4 + [hbm] * peers + [vmem, hbm],
        out_specs=[vmem] * (1 + lines),
        out_shape=[jax.ShapeDtypeStruct((poles, width), F32)]
        + [jax.ShapeDtypeStruct((per_line, poles, width), BF16)] * lines,
        scratch_shapes=[
            pltpu.VMEM((peers, poles, width), BF16),
            pltpu.VMEM((slots, poles, width), BF16),
            pltpu.SemaphoreType.DMA((peers + slots,)),
        ],
        compiler_params=params(0, 16),
        name="slots",
    )(offsets, owners, place, line, *got, rates_wide, local)

    arrived = [picked[0]]
    for d in range(1, lines):
        route = [(i, i ^ d) for i in range(lines)]
        arrived.append(lax.ppermute(picked[d], "ch", route))

    thin = min(width, 8 * LANES)
    output = pl.pallas_call(
        functools.partial(output_kernel, size),
        grid=(width // thin,),
        in_specs=[lanes(length, thin), lanes(length, thin), lanes(poles, thin), lanes(length, thin)],
        out_specs=lanes(length, thin),
        out_shape=jax.ShapeDtypeStruct((length, width), BF16),
        compiler_params=params(1, 52),
        cost_estimate=pl.CostEstimate(
            flops=3 * 512 * length * width, bytes_accessed=12 * length * width, transcendentals=0
        ),
        name="output",
    )(query, local, entering, weight)

    doc_states = pl.pallas_call(
        widen_kernel,
        in_specs=[SMEM] + [vmem] * lines,
        out_specs=vmem,
        out_shape=jax.ShapeDtypeStruct((per_line, poles, lines * width), F32),
        compiler_params=params(0, 16),
        name="widen",
    )(line, *arrived)
    return (output, doc_states)


def solution(mesh):
    placed = (
        P("ctx", "ch"),
        P("ctx", "ch"),
        P("ctx", "ch"),
        P(None, "ch"),
        P(None, "ch"),
        P(None, "ch"),
        P("ch"),
        P(),
        P(),
    )
    return jax.shard_map(
        per_device,
        mesh=mesh,
        in_specs=placed,
        out_specs=(P("ctx", "ch"), P(("ctx", "ch"), None, None)),
        check_vma=False,
    )
```

```python
import functools

import jax
import jax.numpy as jnp
from jax import lax
from jax.experimental import pallas as pl
from jax.experimental.pallas import tpu as pltpu
from jax.sharding import PartitionSpec as P

TAPS = 128
ENDS = 16
LANES = 128
BLOCK = 1024
PART = 512
CHUNK = 32
F32 = jnp.float32
BF16 = jnp.bfloat16

SMEM = pl.BlockSpec(memory_space=pltpu.SMEM)


def params(grid_dims, mebibytes):
    return pltpu.CompilerParams(
        dimension_semantics=("arbitrary",) * grid_dims, vmem_limit_bytes=mebibytes * 1024 * 1024
    )


def iota(shape, dim):
    return lax.broadcasted_iota(jnp.int32, shape, dim)


def dot(a, b):
    return lax.dot_general(a, b, (((1,), (0,)), ((), ())), preferred_element_type=F32)


def dot_t(a, b):
    return lax.dot_general(a, b, (((0,), (0,)), ((), ())), preferred_element_type=F32)


def spread(x, first_group, size, lanes):
    groups = x.shape[1]
    pick = (iota((groups, lanes), 0) == first_group + iota((groups, lanes), 1) // size).astype(F32)
    pick = pick.astype(BF16)
    high = x.astype(BF16)
    rest = x - high.astype(F32)
    mid = rest.astype(BF16)
    low = (rest - mid.astype(F32)).astype(BF16)
    return dot(high, pick) + dot(mid, pick) + dot(low, pick)


def gain(rates):
    x = 2.0 * rates
    tail = 1.0 - x / 9.0
    for k in range(8, 1, -1):
        tail = 1.0 - x * tail * (1.0 / k)
    return jnp.sqrt(x * tail)


def circulant(row):
    return pltpu.roll(
        jnp.broadcast_to(row, (TAPS, TAPS)), 0, 1, stride=1, stride_axis=0
    ).astype(BF16)


def doc_at(offsets, position):
    docs = offsets.shape[0] - 1
    low, high = jnp.int32(0), jnp.int32(docs)
    for _ in range(docs.bit_length()):
        middle = (low + high) // 2
        left = offsets[middle] <= position
        low, high = jnp.where(left, middle, low), jnp.where(left, high, middle)
    return low


def filtered(blocks, masks, earlier, current, window, key):
    lane_group = iota((TAPS, LANES), 1) // (LANES // len(blocks))
    total = jnp.zeros((TAPS, LANES), F32)
    for g, c in enumerate(blocks):
        y = dot(jnp.concatenate([c * masks[earlier], c * masks[current]], axis=1), window)
        total = jnp.where(lane_group == g, y, total)
    return (key.astype(F32) * total).astype(BF16)


def prepare_kernel(
    cap,
    peers,
    size,
    offsets,
    owners,
    place,
    filt,
    rates,
    resid,
    rates_out,
    gains_out,
    rows_out,
    masks_out,
    taps_out,
    keep,
    last,
):
    poles, groups = rates.shape
    width = rates_out.shape[1]
    length = 2 * TAPS
    docs = offsets.shape[0] - 1
    chosen = owners.shape[0]
    begin = place[0] * length
    d0 = doc_at(offsets, begin)

    def clear(t, carry):
        for u in range(8):
            keep[t * 8 + u] = jnp.float32(1.0)
        return carry

    lax.fori_loop(0, length // 8, clear, 0)
    for row in range(peers * cap):
        last[row] = 0

    def mark(k, carry):
        doc = d0 + k
        order = doc - owners[0]
        order = jnp.where(order < 0, order + docs, order)
        start = offsets[jnp.minimum(doc, docs)] - begin
        end = offsets[jnp.minimum(doc + 1, docs)] - 1 - begin

        @pl.when((doc < docs) & (start >= 0) & (start < length))
        def opens():
            keep[start] = jnp.float32(0.0)

        @pl.when((doc < docs) & (end < length) & (order < chosen))
        def closes():
            last[lax.rem(order, peers) * cap + lax.rem(order // peers, cap)] = end

        return carry

    lax.fori_loop(0, ENDS + 1, mark, 0)

    spot = begin + iota((length, LANES), 0)
    starts = jnp.broadcast_to(offsets[d0], (length, LANES))
    for k in range(1, ENDS + 1):
        off = offsets[jnp.minimum(d0 + k, docs)]
        starts = jnp.where(spot >= off, off, starts)
    i, j = iota((TAPS, TAPS), 0), iota((TAPS, TAPS), 1)
    s0, s1 = starts[:TAPS], starts[TAPS:]
    cross = s1 <= begin + j
    for index, mask in enumerate(
        (
            (j > i) & (s0 <= begin - TAPS + j),
            (j <= i) & (s0 <= begin + j),
            (j > i) & cross,
            (j <= i) & (s1 <= begin + TAPS + j),
            (j <= i) & cross,
        )
    ):
        masks_out[index] = mask.astype(F32).astype(BF16)
    turn = (i == (TAPS - j) % TAPS).astype(F32).astype(BF16)
    rows_out[...] = dot_t(filt[...], turn)
    lag = iota((TAPS, groups), 0).astype(F32)
    gains = gain(rates[...])
    weight = resid[...] * gains
    near = jnp.zeros((TAPS, groups), F32)
    far = jnp.zeros((TAPS, groups), F32)
    for n in range(poles):
        term = weight[n : n + 1] * jnp.exp(-rates[n : n + 1] * lag)
        near = near + term
        far = far + term * jnp.exp(-rates[n : n + 1] * float(TAPS))
    taps_out[0] = dot_t(near.astype(BF16), turn)
    taps_out[1] = dot_t(far.astype(BF16), turn)
    for tile in range(width // LANES):
        at = pl.ds(tile * LANES, LANES)
        wide = spread(rates[...], tile * (LANES // size), size, LANES)
        rates_out[:, at] = wide
        gains_out[:, at] = gain(wide)


def second_kernel(size, value, key, rows, masks, kept):
    per_tile = LANES // size
    tiles = value.shape[1] // LANES
    for tile in range(tiles):
        at = slice(tile * LANES, (tile + 1) * LANES)
        blocks = []
        for g in range(tile * per_tile, (tile + 1) * per_tile):
            blocks.append(circulant(rows[g : g + 1]))
            kept[g] = blocks[-1]
        kept[tiles * per_tile + tile] = filtered(blocks, masks, 2, 3, value[:, at], key[:, at])


def states_kernel(
    cap,
    size,
    place,
    keep,
    last,
    halo,
    value,
    key,
    kept,
    masks,
    rates,
    gains,
    mixed_out,
    *rest,
):
    ends_out, (wide, history) = rest[:-2], rest[-2:]
    poles, width = rates.shape
    length, block = 2 * TAPS, value.shape[1]
    peers = len(ends_out)
    step = pl.program_id(0)
    per_tile = LANES // size

    for tile in range(block // LANES):
        at = slice(tile * LANES, (tile + 1) * LANES)
        spot = pl.ds(pl.multiple_of(step * block + tile * LANES, LANES), LANES)
        window = jnp.concatenate([halo[:, at], value[:, at]], axis=0)
        blocks = [kept[tile * per_tile + g] for g in range(per_tile)]
        second = kept[block // LANES * per_tile + tile]
        mixed = filtered(blocks, masks, 0, 1, window, key[:, at])
        mixed_out[:TAPS, at] = mixed
        mixed_out[TAPS:, at] = second
        wide[:TAPS, spot] = mixed.astype(F32)
        wide[TAPS:, spot] = second.astype(F32)

    @pl.when(step == pl.num_programs(0) - 1)
    def run():
        part = history.shape[2]
        for first in range(0, width, part):
            lanes = slice(first, first + part)
            fade = jnp.exp(-rates[:, lanes])

            def some(c, state):
                base = pl.multiple_of(c * CHUNK, CHUNK)
                for t in range(CHUNK):
                    state = (fade * keep[base + t]) * state + wide[pl.ds(base + t, 1), lanes]
                    history[base + t] = state
                return state

            state = lax.fori_loop(0, length // CHUNK, some, jnp.zeros((poles, part), F32))
            scale = gains[:, lanes]
            through = (state * scale).astype(BF16)
            for d in range(peers):
                peer = lax.rem(place[0] + d, peers)
                for i in range(cap):
                    end = history[last[peer * cap + i]]
                    ends_out[d][i, :, lanes] = (end * scale).astype(BF16)
                ends_out[d][cap, :, lanes] = through


def local_kernel(
    size, offsets, place, mixed, masks, taps, skip, rates, resid, local_out, weight_out, limit
):
    length, block = mixed.shape
    begin = place[0] * length
    step = pl.program_id(0)
    per_tile = LANES // size

    @pl.when(step == 0)
    def prepare():
        doc = doc_at(offsets, begin)
        limit[0] = jnp.where(offsets[doc] < begin, offsets[doc + 1] - begin, 0)

    t = iota((length, LANES), 0)
    lane_group = iota((TAPS, LANES), 1) // size
    for tile in range(block // LANES):
        at = slice(tile * LANES, (tile + 1) * LANES)
        x = mixed[:, at]
        acc0 = jnp.zeros((TAPS, LANES), F32)
        acc1 = jnp.zeros((TAPS, LANES), F32)
        for g in range(per_tile):
            row = tile * per_tile + g
            a, b = circulant(taps[0, row : row + 1]), circulant(taps[1, row : row + 1])
            y0 = dot(a * masks[1], x[:TAPS])
            y1 = dot(jnp.concatenate([a * masks[2] + b * masks[4], a * masks[3]], axis=1), x)
            acc0 = jnp.where(lane_group == g, y0, acc0)
            acc1 = jnp.where(lane_group == g, y1, acc1)
        total = jnp.concatenate([acc0, acc1], axis=0) + skip[:, at] * x.astype(F32)
        local_out[:, at] = total.astype(BF16)
        weight = jnp.exp(-rates[:, at] * (t + 1).astype(F32)) * resid[:, at]
        weight = jnp.where(t < limit[0], weight, 0.0)
        weight_out[:, at] = weight.astype(BF16)


def slots_kernel(length, lines, peers, offsets, owners, place, line, *rest):
    got, (rates, after, entering_out) = rest[:peers], rest[peers : peers + 3]
    slot_outs = rest[peers + 3 : peers + 3 + lines]
    through, mine, sems = rest[peers + 3 + lines :]
    cap = got[0].shape[0] - 1
    per_line = slot_outs[0].shape[0]
    me = place[0]
    arriving = []
    for d in range(peers):
        source = lax.rem(me - d + peers, peers)
        arriving.append(pltpu.make_async_copy(got[d].at[cap], through.at[source], sems.at[d]))
        arriving[-1].start()
    spans = []
    for d in range(lines):
        for q in range(per_line):
            k = (line[0] ^ d) * per_line + q
            doc = owners[me * (lines * per_line) + k]
            start, end = offsets[doc], offsets[doc + 1] - 1
            spot = d * per_line + q
            behind = lax.rem(me - end // length + peers, peers)
            for e in range(peers):

                @pl.when(behind == e)
                def fetch(e=e, k=k, spot=spot):
                    pltpu.make_async_copy(
                        got[e].at[lax.rem(k, cap)], mine.at[spot], sems.at[peers + spot]
                    ).start()

            spans.append((start, end))
    p = rates[...]
    fade = jnp.exp(-p * float(length))

    def entering(first, stop):
        def hop(c, state):
            return fade * state + through[c].astype(F32)

        return lax.fori_loop(first, stop, hop, jnp.zeros(p.shape, F32))

    my_start = offsets[doc_at(offsets, me * length)]
    for copy in arriving:
        copy.wait()
    for spot, (start, end) in enumerate(spans):
        source = end // length
        link = jnp.exp(-p * (end - source * length + 1).astype(F32))
        extra = link * entering(start // length, source)
        pltpu.make_async_copy(got[0].at[0], mine.at[spot], sems.at[peers + spot]).wait()
        state = mine[spot].astype(F32) + extra
        slot_outs[spot // per_line][spot % per_line] = state.astype(BF16)
    entering_out[...] = entering(my_start // length, me)


def output_kernel(size, query, local, entering, weight, out):
    poles, width = entering.shape
    tile = 2 * LANES
    kept = iota((tile, tile), 0) // poles == iota((tile, tile), 1) // size
    kept = kept.astype(F32).astype(BF16)
    for first in range(0, width, tile):
        at = slice(first, first + tile)
        spread_out = jnp.concatenate([entering[:, at].astype(BF16)] * (tile // size), axis=0) * kept
        fix = dot(weight[:, at], spread_out)
        out[:, at] = (query[:, at].astype(F32) * (local[:, at].astype(F32) + fix)).astype(BF16)


def widen_kernel(line, *refs):
    parts, out = refs[:-1], refs[-1]
    width = parts[0].shape[2]
    for d, part in enumerate(parts):
        source = line[0] ^ d
        out[:, :, pl.ds(pl.multiple_of(source * width, width), width)] = part[...].astype(F32)


def per_device(query, key, value, filt, rates, resid, skip, offsets, owners):
    length, width = value.shape
    poles, groups = rates.shape
    size = width // groups
    peers, lines = lax.axis_size("ctx"), lax.axis_size("ch")
    slots = owners.shape[0] // peers
    cap = -(-ENDS // peers)
    line = lax.axis_index("ch").astype(jnp.int32).reshape(1)
    place = lax.axis_index("ctx").astype(jnp.int32).reshape(1)
    rates_flat = rates.T.reshape(1, groups * poles)
    resid_flat = resid.T.reshape(1, groups * poles)

    halo = lax.ppermute(
        value[length - TAPS :], "ctx", [(i, i + 1) for i in range(peers - 1)]
    )

    def whole(shape):
        return pl.BlockSpec(shape, lambda i: (0,) * len(shape))

    block = min(width, BLOCK)

    def lanes(height, size=block):
        return pl.BlockSpec((height, size), lambda i: (0, i))

    vmem = pl.BlockSpec(memory_space=pltpu.VMEM)
    hbm = pl.BlockSpec(memory_space=pl.ANY)
    rates_wide, gains_wide, rows, masks, taps, keep, last = pl.pallas_call(
        functools.partial(prepare_kernel, cap, peers, size),
        in_specs=[SMEM] * 3 + [vmem] * 3,
        out_specs=[vmem] * 5 + [SMEM] * 2,
        out_shape=[
            jax.ShapeDtypeStruct((poles, width), F32),
            jax.ShapeDtypeStruct((poles, width), F32),
            jax.ShapeDtypeStruct((groups, TAPS), F32),
            jax.ShapeDtypeStruct((5, TAPS, TAPS), BF16),
            jax.ShapeDtypeStruct((2, groups, TAPS), F32),
            jax.ShapeDtypeStruct((length,), F32),
            jax.ShapeDtypeStruct((peers * cap,), jnp.int32),
        ],
        compiler_params=params(0, 60),
        cost_estimate=pl.CostEstimate(flops=1 << 30, bytes_accessed=1 << 20, transcendentals=0),
        name="prepare",
    )(offsets, owners, place, filt, rates, resid)

    def half(row, size=block):
        return pl.BlockSpec((TAPS, size), lambda i: (row, i))

    entries = block // size + block // LANES
    kept = pl.pallas_call(
        functools.partial(second_kernel, size),
        grid=(width // block,),
        in_specs=[
            lanes(length),
            half(1),
            pl.BlockSpec((block // size, TAPS), lambda i: (i, 0)),
            whole((5, TAPS, TAPS)),
        ],
        out_specs=pl.BlockSpec((entries, TAPS, TAPS), lambda i: (i, 0, 0)),
        out_shape=jax.ShapeDtypeStruct((width // block * entries, TAPS, TAPS), BF16),
        compiler_params=params(1, 60),
        cost_estimate=pl.CostEstimate(
            flops=16 * length * length * width, bytes_accessed=7 * length * width, transcendentals=0
        ),
        name="second",
    )(value, key, rows, masks)

    mixed, *ends = pl.pallas_call(
        functools.partial(states_kernel, cap, size),
        grid=(width // block,),
        in_specs=[
            SMEM,
            SMEM,
            SMEM,
            half(0),
            half(0),
            half(0),
            pl.BlockSpec((entries, TAPS, TAPS), lambda i: (i, 0, 0)),
            whole((5, TAPS, TAPS)),
            whole((poles, width)),
            whole((poles, width)),
        ],
        out_specs=[lanes(length)] + [whole((cap + 1, poles, width))] * peers,
        out_shape=[jax.ShapeDtypeStruct((length, width), BF16)]
        + [jax.ShapeDtypeStruct((cap + 1, poles, width), BF16)] * peers,
        scratch_shapes=[
            pltpu.VMEM((length, width), F32),
            pltpu.VMEM((length, poles, min(block, PART)), F32),
        ],
        compiler_params=params(1, 50),
        name="states",
    )(place, keep, last, halo, value, key, kept, masks, rates_wide, gains_wide)

    got = [ends[0]]
    for d in range(1, peers):
        route = [(i, (i + d) % peers) for i in range(peers)]
        got.append(lax.ppermute(ends[d], "ctx", route))

    broad = min(width, 8 * LANES)
    local, weight = pl.pallas_call(
        functools.partial(local_kernel, size),
        grid=(width // broad,),
        in_specs=[
            SMEM,
            SMEM,
            lanes(length, broad),
            whole((5, TAPS, TAPS)),
            pl.BlockSpec((2, broad // size, TAPS), lambda i: (0, i, 0)),
            lanes(1, broad),
            lanes(1, broad),
            lanes(1, broad),
        ],
        out_specs=[lanes(length, broad)] * 2,
        out_shape=[
            jax.ShapeDtypeStruct((length, width), BF16),
            jax.ShapeDtypeStruct((length, width), BF16),
        ],
        scratch_shapes=[pltpu.SMEM((1,), jnp.int32)],
        compiler_params=params(1, 48),
        cost_estimate=pl.CostEstimate(
            flops=32 * length * length * width, bytes_accessed=6 * length * width, transcendentals=0
        ),
        name="local",
    )(offsets, place, mixed, masks, taps, skip.reshape(1, width), rates_flat, resid_flat)

    per_line = slots // lines
    entering, *picked = pl.pallas_call(
        functools.partial(slots_kernel, length, lines, peers),
        in_specs=[SMEM] * 4 + [hbm] * peers + [vmem, hbm],
        out_specs=[vmem] * (1 + lines),
        out_shape=[jax.ShapeDtypeStruct((poles, width), F32)]
        + [jax.ShapeDtypeStruct((per_line, poles, width), BF16)] * lines,
        scratch_shapes=[
            pltpu.VMEM((peers, poles, width), BF16),
            pltpu.VMEM((slots, poles, width), BF16),
            pltpu.SemaphoreType.DMA((peers + slots,)),
        ],
        compiler_params=params(0, 16),
        name="slots",
    )(offsets, owners, place, line, *got, rates_wide, local)

    arrived = [picked[0]]
    for d in range(1, lines):
        route = [(i, i ^ d) for i in range(lines)]
        arrived.append(lax.ppermute(picked[d], "ch", route))

    thin = min(width, 8 * LANES)
    output = pl.pallas_call(
        functools.partial(output_kernel, size),
        grid=(width // thin,),
        in_specs=[lanes(length, thin), lanes(length, thin), lanes(poles, thin), lanes(length, thin)],
        out_specs=lanes(length, thin),
        out_shape=jax.ShapeDtypeStruct((length, width), BF16),
        compiler_params=params(1, 52),
        cost_estimate=pl.CostEstimate(
            flops=3 * 512 * length * width, bytes_accessed=12 * length * width, transcendentals=0
        ),
        name="output",
    )(query, local, entering, weight)

    doc_states = pl.pallas_call(
        widen_kernel,
        in_specs=[SMEM] + [vmem] * lines,
        out_specs=vmem,
        out_shape=jax.ShapeDtypeStruct((per_line, poles, lines * width), F32),
        compiler_params=params(0, 16),
        name="widen",
    )(line, *arrived)
    return (output, doc_states)


def solution(mesh):
    placed = (
        P("ctx", "ch"),
        P("ctx", "ch"),
        P("ctx", "ch"),
        P(None, "ch"),
        P(None, "ch"),
        P(None, "ch"),
        P("ch"),
        P(),
        P(),
    )
    return jax.shard_map(
        per_device,
        mesh=mesh,
        in_specs=placed,
        out_specs=(P("ctx", "ch"), P(("ctx", "ch"), None, None)),
        check_vma=False,
    )
```

```python
import functools

import jax
import jax.numpy as jnp
from jax import lax
from jax.experimental import pallas as pl
from jax.experimental.pallas import tpu as pltpu
from jax.sharding import PartitionSpec as P

TAPS = 128
ENDS = 16
LANES = 128
BLOCK = 1024
PART = 512
CHUNK = 64
F32 = jnp.float32
BF16 = jnp.bfloat16

SMEM = pl.BlockSpec(memory_space=pltpu.SMEM)


def params(grid_dims, mebibytes):
    return pltpu.CompilerParams(
        dimension_semantics=("arbitrary",) * grid_dims, vmem_limit_bytes=mebibytes * 1024 * 1024
    )


def iota(shape, dim):
    return lax.broadcasted_iota(jnp.int32, shape, dim)


def dot(a, b):
    return lax.dot_general(a, b, (((1,), (0,)), ((), ())), preferred_element_type=F32)


def dot_t(a, b):
    return lax.dot_general(a, b, (((0,), (0,)), ((), ())), preferred_element_type=F32)


def spread(x, first_group, size, lanes):
    groups = x.shape[1]
    pick = (iota((groups, lanes), 0) == first_group + iota((groups, lanes), 1) // size).astype(F32)
    pick = pick.astype(BF16)
    high = x.astype(BF16)
    rest = x - high.astype(F32)
    mid = rest.astype(BF16)
    low = (rest - mid.astype(F32)).astype(BF16)
    return dot(high, pick) + dot(mid, pick) + dot(low, pick)


def gain(rates):
    x = 2.0 * rates
    tail = 1.0 - x / 9.0
    for k in range(8, 1, -1):
        tail = 1.0 - x * tail * (1.0 / k)
    return jnp.sqrt(x * tail)


def circulant(row):
    return pltpu.roll(
        jnp.broadcast_to(row, (TAPS, TAPS)), 0, 1, stride=1, stride_axis=0
    ).astype(BF16)


def doc_at(offsets, position):
    docs = offsets.shape[0] - 1
    low, high = jnp.int32(0), jnp.int32(docs)
    for _ in range(docs.bit_length()):
        middle = (low + high) // 2
        left = offsets[middle] <= position
        low, high = jnp.where(left, middle, low), jnp.where(left, high, middle)
    return low


def filtered(blocks, masks, earlier, current, window, key):
    lane_group = iota((TAPS, LANES), 1) // (LANES // len(blocks))
    total = jnp.zeros((TAPS, LANES), F32)
    for g, c in enumerate(blocks):
        y = dot(jnp.concatenate([c * masks[earlier], c * masks[current]], axis=1), window)
        total = jnp.where(lane_group == g, y, total)
    return (key.astype(F32) * total).astype(BF16)


def prepare_kernel(
    cap,
    peers,
    size,
    offsets,
    owners,
    place,
    filt,
    rates,
    resid,
    rates_out,
    gains_out,
    rows_out,
    masks_out,
    taps_out,
    keep,
    last,
):
    poles, groups = rates.shape
    width = rates_out.shape[1]
    length = 2 * TAPS
    docs = offsets.shape[0] - 1
    chosen = owners.shape[0]
    begin = place[0] * length
    d0 = doc_at(offsets, begin)

    def clear(t, carry):
        for u in range(8):
            keep[t * 8 + u] = jnp.float32(1.0)
        return carry

    lax.fori_loop(0, length // 8, clear, 0)
    for row in range(peers * cap):
        last[row] = 0

    def mark(k, carry):
        doc = d0 + k
        order = doc - owners[0]
        order = jnp.where(order < 0, order + docs, order)
        start = offsets[jnp.minimum(doc, docs)] - begin
        end = offsets[jnp.minimum(doc + 1, docs)] - 1 - begin

        @pl.when((doc < docs) & (start >= 0) & (start < length))
        def opens():
            keep[start] = jnp.float32(0.0)

        @pl.when((doc < docs) & (end < length) & (order < chosen))
        def closes():
            last[lax.rem(order, peers) * cap + lax.rem(order // peers, cap)] = end

        return carry

    lax.fori_loop(0, ENDS + 1, mark, 0)

    spot = begin + iota((length, LANES), 0)
    starts = jnp.broadcast_to(offsets[d0], (length, LANES))
    for k in range(1, ENDS + 1):
        off = offsets[jnp.minimum(d0 + k, docs)]
        starts = jnp.where(spot >= off, off, starts)
    i, j = iota((TAPS, TAPS), 0), iota((TAPS, TAPS), 1)
    s0, s1 = starts[:TAPS], starts[TAPS:]
    cross = s1 <= begin + j
    for index, mask in enumerate(
        (
            (j > i) & (s0 <= begin - TAPS + j),
            (j <= i) & (s0 <= begin + j),
            (j > i) & cross,
            (j <= i) & (s1 <= begin + TAPS + j),
            (j <= i) & cross,
        )
    ):
        masks_out[index] = mask.astype(F32).astype(BF16)
    turn = (i == (TAPS - j) % TAPS).astype(F32).astype(BF16)
    rows_out[...] = dot_t(filt[...], turn)
    lag = iota((TAPS, groups), 0).astype(F32)
    gains = gain(rates[...])
    weight = resid[...] * gains
    near = jnp.zeros((TAPS, groups), F32)
    far = jnp.zeros((TAPS, groups), F32)
    for n in range(poles):
        term = weight[n : n + 1] * jnp.exp(-rates[n : n + 1] * lag)
        near = near + term
        far = far + term * jnp.exp(-rates[n : n + 1] * float(TAPS))
    taps_out[0] = dot_t(near.astype(BF16), turn)
    taps_out[1] = dot_t(far.astype(BF16), turn)
    for tile in range(width // LANES):
        at = pl.ds(tile * LANES, LANES)
        wide = spread(rates[...], tile * (LANES // size), size, LANES)
        rates_out[:, at] = wide
        gains_out[:, at] = gain(wide)


def second_kernel(size, value, key, rows, masks, kept):
    per_tile = LANES // size
    tiles = value.shape[1] // LANES
    for tile in range(tiles):
        at = slice(tile * LANES, (tile + 1) * LANES)
        blocks = []
        for g in range(tile * per_tile, (tile + 1) * per_tile):
            blocks.append(circulant(rows[g : g + 1]))
            kept[g] = blocks[-1]
        kept[tiles * per_tile + tile] = filtered(blocks, masks, 2, 3, value[:, at], key[:, at])


def states_kernel(
    cap,
    size,
    place,
    keep,
    last,
    halo,
    value,
    key,
    kept,
    masks,
    rates,
    gains,
    mixed_out,
    *rest,
):
    ends_out, (wide, history) = rest[:-2], rest[-2:]
    poles, width = rates.shape
    length, block = 2 * TAPS, value.shape[1]
    peers = len(ends_out)
    step = pl.program_id(0)
    per_tile = LANES // size

    for tile in range(block // LANES):
        at = slice(tile * LANES, (tile + 1) * LANES)
        spot = pl.ds(pl.multiple_of(step * block + tile * LANES, LANES), LANES)
        window = jnp.concatenate([halo[:, at], value[:, at]], axis=0)
        blocks = [kept[tile * per_tile + g] for g in range(per_tile)]
        second = kept[block // LANES * per_tile + tile]
        mixed = filtered(blocks, masks, 0, 1, window, key[:, at])
        mixed_out[:TAPS, at] = mixed
        mixed_out[TAPS:, at] = second
        wide[:TAPS, spot] = mixed.astype(F32)
        wide[TAPS:, spot] = second.astype(F32)

    @pl.when(step == pl.num_programs(0) - 1)
    def run():
        part = history.shape[2]
        for first in range(0, width, part):
            lanes = slice(first, first + part)
            fade = jnp.exp(-rates[:, lanes])

            def some(c, state):
                base = pl.multiple_of(c * CHUNK, CHUNK)
                for t in range(CHUNK):
                    state = (fade * keep[base + t]) * state + wide[pl.ds(base + t, 1), lanes]
                    history[base + t] = state
                return state

            state = lax.fori_loop(0, length // CHUNK, some, jnp.zeros((poles, part), F32))
            scale = gains[:, lanes]
            through = (state * scale).astype(BF16)
            for d in range(peers):
                peer = lax.rem(place[0] + d, peers)
                for i in range(cap):
                    end = history[last[peer * cap + i]]
                    ends_out[d][i, :, lanes] = (end * scale).astype(BF16)
                ends_out[d][cap, :, lanes] = through


def local_kernel(
    size, offsets, place, mixed, masks, taps, skip, rates, resid, local_out, weight_out, limit
):
    length, block = mixed.shape
    begin = place[0] * length
    step = pl.program_id(0)
    per_tile = LANES // size

    @pl.when(step == 0)
    def prepare():
        doc = doc_at(offsets, begin)
        limit[0] = jnp.where(offsets[doc] < begin, offsets[doc + 1] - begin, 0)

    t = iota((length, LANES), 0)
    lane_group = iota((TAPS, LANES), 1) // size
    for tile in range(block // LANES):
        at = slice(tile * LANES, (tile + 1) * LANES)
        x = mixed[:, at]
        acc0 = jnp.zeros((TAPS, LANES), F32)
        acc1 = jnp.zeros((TAPS, LANES), F32)
        for g in range(per_tile):
            row = tile * per_tile + g
            a, b = circulant(taps[0, row : row + 1]), circulant(taps[1, row : row + 1])
            y0 = dot(a * masks[1], x[:TAPS])
            y1 = dot(jnp.concatenate([a * masks[2] + b * masks[4], a * masks[3]], axis=1), x)
            acc0 = jnp.where(lane_group == g, y0, acc0)
            acc1 = jnp.where(lane_group == g, y1, acc1)
        total = jnp.concatenate([acc0, acc1], axis=0) + skip[:, at] * x.astype(F32)
        local_out[:, at] = total.astype(BF16)
        weight = jnp.exp(-rates[:, at] * (t + 1).astype(F32)) * resid[:, at]
        weight = jnp.where(t < limit[0], weight, 0.0)
        weight_out[:, at] = weight.astype(BF16)


def slots_kernel(length, lines, peers, offsets, owners, place, line, *rest):
    got, (rates, after, entering_out) = rest[:peers], rest[peers : peers + 3]
    slot_outs = rest[peers + 3 : peers + 3 + lines]
    through, mine, sems = rest[peers + 3 + lines :]
    cap = got[0].shape[0] - 1
    per_line = slot_outs[0].shape[0]
    me = place[0]
    arriving = []
    for d in range(peers):
        source = lax.rem(me - d + peers, peers)
        arriving.append(pltpu.make_async_copy(got[d].at[cap], through.at[source], sems.at[d]))
        arriving[-1].start()
    spans = []
    for d in range(lines):
        for q in range(per_line):
            k = (line[0] ^ d) * per_line + q
            doc = owners[me * (lines * per_line) + k]
            start, end = offsets[doc], offsets[doc + 1] - 1
            spot = d * per_line + q
            behind = lax.rem(me - end // length + peers, peers)
            for e in range(peers):

                @pl.when(behind == e)
                def fetch(e=e, k=k, spot=spot):
                    pltpu.make_async_copy(
                        got[e].at[lax.rem(k, cap)], mine.at[spot], sems.at[peers + spot]
                    ).start()

            spans.append((start, end))
    p = rates[...]
    fade = jnp.exp(-p * float(length))

    def entering(first, stop):
        def hop(c, state):
            return fade * state + through[c].astype(F32)

        return lax.fori_loop(first, stop, hop, jnp.zeros(p.shape, F32))

    my_start = offsets[doc_at(offsets, me * length)]
    for copy in arriving:
        copy.wait()
    for spot, (start, end) in enumerate(spans):
        source = end // length
        link = jnp.exp(-p * (end - source * length + 1).astype(F32))
        extra = link * entering(start // length, source)
        pltpu.make_async_copy(got[0].at[0], mine.at[spot], sems.at[peers + spot]).wait()
        state = mine[spot].astype(F32) + extra
        slot_outs[spot // per_line][spot % per_line] = state.astype(BF16)
    entering_out[...] = entering(my_start // length, me)


def output_kernel(size, query, local, entering, weight, out):
    poles, width = entering.shape
    tile = 2 * LANES
    kept = iota((tile, tile), 0) // poles == iota((tile, tile), 1) // size
    kept = kept.astype(F32).astype(BF16)
    for first in range(0, width, tile):
        at = slice(first, first + tile)
        spread_out = jnp.concatenate([entering[:, at].astype(BF16)] * (tile // size), axis=0) * kept
        fix = dot(weight[:, at], spread_out)
        out[:, at] = (query[:, at].astype(F32) * (local[:, at].astype(F32) + fix)).astype(BF16)


def widen_kernel(line, *refs):
    parts, out = refs[:-1], refs[-1]
    width = parts[0].shape[2]
    for d, part in enumerate(parts):
        source = line[0] ^ d
        out[:, :, pl.ds(pl.multiple_of(source * width, width), width)] = part[...].astype(F32)


def per_device(query, key, value, filt, rates, resid, skip, offsets, owners):
    length, width = value.shape
    poles, groups = rates.shape
    size = width // groups
    peers, lines = lax.axis_size("ctx"), lax.axis_size("ch")
    slots = owners.shape[0] // peers
    cap = -(-ENDS // peers)
    line = lax.axis_index("ch").astype(jnp.int32).reshape(1)
    place = lax.axis_index("ctx").astype(jnp.int32).reshape(1)
    rates_flat = rates.T.reshape(1, groups * poles)
    resid_flat = resid.T.reshape(1, groups * poles)

    halo = lax.ppermute(
        value[length - TAPS :], "ctx", [(i, i + 1) for i in range(peers - 1)]
    )

    def whole(shape):
        return pl.BlockSpec(shape, lambda i: (0,) * len(shape))

    block = min(width, BLOCK)

    def lanes(height, size=block):
        return pl.BlockSpec((height, size), lambda i: (0, i))

    vmem = pl.BlockSpec(memory_space=pltpu.VMEM)
    hbm = pl.BlockSpec(memory_space=pl.ANY)
    rates_wide, gains_wide, rows, masks, taps, keep, last = pl.pallas_call(
        functools.partial(prepare_kernel, cap, peers, size),
        in_specs=[SMEM] * 3 + [vmem] * 3,
        out_specs=[vmem] * 5 + [SMEM] * 2,
        out_shape=[
            jax.ShapeDtypeStruct((poles, width), F32),
            jax.ShapeDtypeStruct((poles, width), F32),
            jax.ShapeDtypeStruct((groups, TAPS), F32),
            jax.ShapeDtypeStruct((5, TAPS, TAPS), BF16),
            jax.ShapeDtypeStruct((2, groups, TAPS), F32),
            jax.ShapeDtypeStruct((length,), F32),
            jax.ShapeDtypeStruct((peers * cap,), jnp.int32),
        ],
        compiler_params=params(0, 60),
        cost_estimate=pl.CostEstimate(flops=1 << 30, bytes_accessed=1 << 20, transcendentals=0),
        name="prepare",
    )(offsets, owners, place, filt, rates, resid)

    def half(row, size=block):
        return pl.BlockSpec((TAPS, size), lambda i: (row, i))

    entries = block // size + block // LANES
    kept = pl.pallas_call(
        functools.partial(second_kernel, size),
        grid=(width // block,),
        in_specs=[
            lanes(length),
            half(1),
            pl.BlockSpec((block // size, TAPS), lambda i: (i, 0)),
            whole((5, TAPS, TAPS)),
        ],
        out_specs=pl.BlockSpec((entries, TAPS, TAPS), lambda i: (i, 0, 0)),
        out_shape=jax.ShapeDtypeStruct((width // block * entries, TAPS, TAPS), BF16),
        compiler_params=params(1, 60),
        cost_estimate=pl.CostEstimate(
            flops=16 * length * length * width, bytes_accessed=7 * length * width, transcendentals=0
        ),
        name="second",
    )(value, key, rows, masks)

    mixed, *ends = pl.pallas_call(
        functools.partial(states_kernel, cap, size),
        grid=(width // block,),
        in_specs=[
            SMEM,
            SMEM,
            SMEM,
            half(0),
            half(0),
            half(0),
            pl.BlockSpec((entries, TAPS, TAPS), lambda i: (i, 0, 0)),
            whole((5, TAPS, TAPS)),
            whole((poles, width)),
            whole((poles, width)),
        ],
        out_specs=[lanes(length)] + [whole((cap + 1, poles, width))] * peers,
        out_shape=[jax.ShapeDtypeStruct((length, width), BF16)]
        + [jax.ShapeDtypeStruct((cap + 1, poles, width), BF16)] * peers,
        scratch_shapes=[
            pltpu.VMEM((length, width), F32),
            pltpu.VMEM((length, poles, min(block, PART)), F32),
        ],
        compiler_params=params(1, 50),
        name="states",
    )(place, keep, last, halo, value, key, kept, masks, rates_wide, gains_wide)

    got = [ends[0]]
    for d in range(1, peers):
        route = [(i, (i + d) % peers) for i in range(peers)]
        got.append(lax.ppermute(ends[d], "ctx", route))

    broad = min(width, 8 * LANES)
    local, weight = pl.pallas_call(
        functools.partial(local_kernel, size),
        grid=(width // broad,),
        in_specs=[
            SMEM,
            SMEM,
            lanes(length, broad),
            whole((5, TAPS, TAPS)),
            pl.BlockSpec((2, broad // size, TAPS), lambda i: (0, i, 0)),
            lanes(1, broad),
            lanes(1, broad),
            lanes(1, broad),
        ],
        out_specs=[lanes(length, broad)] * 2,
        out_shape=[
            jax.ShapeDtypeStruct((length, width), BF16),
            jax.ShapeDtypeStruct((length, width), BF16),
        ],
        scratch_shapes=[pltpu.SMEM((1,), jnp.int32)],
        compiler_params=params(1, 48),
        cost_estimate=pl.CostEstimate(
            flops=32 * length * length * width, bytes_accessed=6 * length * width, transcendentals=0
        ),
        name="local",
    )(offsets, place, mixed, masks, taps, skip.reshape(1, width), rates_flat, resid_flat)

    per_line = slots // lines
    entering, *picked = pl.pallas_call(
        functools.partial(slots_kernel, length, lines, peers),
        in_specs=[SMEM] * 4 + [hbm] * peers + [vmem, hbm],
        out_specs=[vmem] * (1 + lines),
        out_shape=[jax.ShapeDtypeStruct((poles, width), F32)]
        + [jax.ShapeDtypeStruct((per_line, poles, width), BF16)] * lines,
        scratch_shapes=[
            pltpu.VMEM((peers, poles, width), BF16),
            pltpu.VMEM((slots, poles, width), BF16),
            pltpu.SemaphoreType.DMA((peers + slots,)),
        ],
        compiler_params=params(0, 16),
        name="slots",
    )(offsets, owners, place, line, *got, rates_wide, local)

    arrived = [picked[0]]
    for d in range(1, lines):
        route = [(i, i ^ d) for i in range(lines)]
        arrived.append(lax.ppermute(picked[d], "ch", route))

    thin = min(width, 8 * LANES)
    output = pl.pallas_call(
        functools.partial(output_kernel, size),
        grid=(width // thin,),
        in_specs=[lanes(length, thin), lanes(length, thin), lanes(poles, thin), lanes(length, thin)],
        out_specs=lanes(length, thin),
        out_shape=jax.ShapeDtypeStruct((length, width), BF16),
        compiler_params=params(1, 52),
        cost_estimate=pl.CostEstimate(
            flops=3 * 512 * length * width, bytes_accessed=12 * length * width, transcendentals=0
        ),
        name="output",
    )(query, local, entering, weight)

    doc_states = pl.pallas_call(
        widen_kernel,
        in_specs=[SMEM] + [vmem] * lines,
        out_specs=vmem,
        out_shape=jax.ShapeDtypeStruct((per_line, poles, lines * width), F32),
        compiler_params=params(0, 16),
        name="widen",
    )(line, *arrived)
    return (output, doc_states)


def solution(mesh):
    placed = (
        P("ctx", "ch"),
        P("ctx", "ch"),
        P("ctx", "ch"),
        P(None, "ch"),
        P(None, "ch"),
        P(None, "ch"),
        P("ch"),
        P(),
        P(),
    )
    return jax.shard_map(
        per_device,
        mesh=mesh,
        in_specs=placed,
        out_specs=(P("ctx", "ch"), P(("ctx", "ch"), None, None)),
        check_vma=False,
    )
```
